128 devices in a mesh: pair: 32 (over z, x, core), atom: 4 (over y).
Axes of the slice: x: 4, y: 4, z: 4, core: 2. Of those that a mesh axis runs over, the one named last changes fastest.
Arguments:
- pair_state: bfloat16 [512, 512, 128], P('pair', 'atom'), may hold values from -6 to 6
- cotangent: bfloat16 [512, 512, 128], P('pair', 'atom'), may hold values from -6 to 6
- atom_feats: bfloat16 [16384, 128], P(('pair', 'atom')), may hold values from -6 to 6
- atom_token: int32 [16384], P(('pair', 'atom')), may hold values from 0 to 511, as said below
- window_count: int32 [512], P(('pair', 'atom')), may hold values from 24 to 32, as said below
- input_weight: bfloat16 [128, 640], replicated, may hold values from -0.5 to 0.5
- output_weight: bfloat16 [128, 128], replicated, may hold values from -0.5 to 0.5
- atom_weight: bfloat16 [128, 384], replicated, may hold values from -0.5 to 0.5
- left_weight: bfloat16 [384, 128], replicated, may hold values from -0.3125 to 0.3125
- right_weight: bfloat16 [384, 128], replicated, may hold values from -0.3125 to 0.3125
Outputs:
- pair_grad: bfloat16 [512, 512, 128], P('pair', 'atom')
- atom_grad: bfloat16 [16384, 128], P(('pair', 'atom'))
The draws below stay inside these ranges and needn't reach their ends.
Inputs may be any that keep to these rules, and one draw needn't show every extreme that they name: `atom_token`: taken in slot order, the live slots' tokens never fall, and every token from 0 to 511 is the token of at least one live slot. The device at position d of pair+atom holds slots d * 128 to (d + 1) * 128 - 1; its live slots belong to tokens d * 4 to (d + 1) * 4 - 1, except on every device but the first a leading run of one to four live slots that belong to token d * 4 - 1. A dead slot carries the token of the live slot before it. `window_count`: window 0 is full and window 1 holds exactly 24 live slots in every draw.
All inputs are finite; a program needn't handle non-finite values.
Results may differ from the reference program's by a relative error of at most 0.015.
Values may be sent and summed in bfloat16 or wider, within the bound.
A program may use at most 64 MiB of HBM per device.

```python
import jax
import jax.numpy as jnp
from jax import lax

C = 128
CH = 128
CS = 384
CA = 128
WIN = 32
ROWS = 16
N = 512
TOK_DEV = 4
SLOT_DEV = 128
WINDOWS = 512
ATOMS = 16384
N_PAIR = 32


def shared_counts(key):
    counts = jax.random.randint(jax.random.fold_in(key, 11), (WINDOWS,), 24, WIN + 1)
    return counts.at[0].set(WIN).at[1].set(24).astype(jnp.int32)


def draw_window_count(key, part):
    return shared_counts(key)


def draw_atom_token(key, part):
    counts = shared_counts(key)
    key = jax.random.fold_in(key, 7)
    blocks = ATOMS // SLOT_DEV
    live = (jnp.arange(WIN)[None, :] < counts[:, None]).astype(jnp.int32).reshape(blocks, SLOT_DEV)
    rank = jnp.cumsum(live, axis=1) - 1
    total = jnp.sum(live, axis=1)
    lead_key, weight_key = jax.random.split(key)
    lead = jax.random.randint(lead_key, (blocks,), 1, 5).astype(jnp.int32)
    lead = lead.at[0].set(0)
    weights = jax.random.randint(weight_key, (blocks, TOK_DEV), 1, 9).astype(jnp.int32)
    before = jnp.cumsum(weights, axis=1) - weights
    weight_total = jnp.sum(weights, axis=1)
    extra = total - lead - TOK_DEV
    starts = lead[:, None] + jnp.arange(TOK_DEV, dtype=jnp.int32)[None, :] + before * extra[:, None] // weight_total[:, None]
    local = jnp.sum((starts[:, None, :] <= rank[:, :, None]).astype(jnp.int32), axis=2) - 1
    first = (jnp.arange(blocks, dtype=jnp.int32) * TOK_DEV)[:, None]
    tokens = jnp.where(rank < lead[:, None], first - 1, first + local)
    return tokens.reshape(ATOMS).astype(jnp.int32)


def shard_levels(stream_key, shape, cuts, low, high):
    loudness = 1.0
    for dim, blocks in cuts:
        draws = jax.random.uniform(jax.random.fold_in(jax.random.fold_in(stream_key, 6), dim), (blocks,), jnp.float32, low / len(cuts), high / len(cuts))
        loudness = loudness * jnp.repeat(jnp.exp(draws), shape[dim] // blocks).reshape((-1,) + (1,) * (len(shape) - 1 - dim))
    return loudness


def centred(stream_key, extent, deviation, reach, shards=(), kind=jnp.bfloat16):
    loudness = shard_levels(stream_key, extent, shards, -0.22, 0.18) if shards else 1.0
    result = jax.random.normal(stream_key, extent, jnp.float32) * deviation * loudness
    return jnp.minimum(jnp.maximum(result, -reach), reach).astype(kind)


def setup_inputs(seed: int = 0) -> dict:
    key_of = jax.random.split(jax.random.key(seed), 11)
    return {
        "pair_state": centred(key_of[0], (N, N, C), 1.0, 6.0, ((0, 32), (1, 4))),
        "cotangent": centred(key_of[1], (N, N, C), 1.0, 6.0, ((0, 32), (1, 4))),
        "atom_feats": centred(key_of[2], (ATOMS, CA), 1.0, 6.0, ((0, 128),)),
        "atom_token": draw_atom_token(jax.random.fold_in(key_of[10], 71), 0),
        "window_count": draw_window_count(jax.random.fold_in(key_of[10], 71), 0),
        "input_weight": centred(key_of[5], (C, 4 * CH + C), C ** -0.5, 0.5),
        "output_weight": centred(key_of[6], (CH, C), CH ** -0.5, 0.5),
        "atom_weight": centred(key_of[7], (CA, CS), CA ** -0.5, 0.5),
        "left_weight": centred(key_of[8], (CS, C), CS ** -0.5, 0.3125),
        "right_weight": centred(key_of[9], (CS, C), CS ** -0.5, 0.3125),
    }


EPSILON = 1e-05
HIGHEST = lax.Precision.HIGHEST

def layer_stats(values, axis):
    centre = lax.optimization_barrier(jnp.mean(values, axis=axis, keepdims=True))
    shifted = values - centre
    inverse = lax.rsqrt(lax.optimization_barrier(jnp.mean(shifted * shifted, axis=axis, keepdims=True)) + EPSILON)
    return (shifted * inverse, inverse)

def layer_backward(upstream, normed, inverse, axis):
    first_mean = lax.optimization_barrier(jnp.mean(upstream, axis=axis, keepdims=True))
    cross_mean = lax.optimization_barrier(jnp.mean(upstream * normed, axis=axis, keepdims=True))
    return inverse * (upstream - first_mean - normed * cross_mean)

def rounded(values):
    return lax.optimization_barrier(values.astype(jnp.bfloat16)).astype(jnp.float32)

def pair_front(pair_rows, left_rows, right_bias, input_weight):
    inputs = pair_rows.astype(jnp.float32) + left_rows.astype(jnp.float32)[:, None, :] + right_bias.astype(jnp.float32)[None, :, :]
    normed, inverse = layer_stats(inputs, -1)
    hidden_in = rounded(normed)
    weights = input_weight.astype(jnp.float32)
    values = [jnp.einsum('rkc,ch->hrk', hidden_in, weights[:, quarter * CH:(quarter + 1) * CH]) for quarter in range(4)]
    gate_pre = jnp.einsum('rkc,cd->rkd', hidden_in, weights[:, 4 * CH:])
    return (normed, inverse, values, gate_pre)

def edge_values(values):
    left_edge = (jax.nn.sigmoid(values[1]) * values[0]).astype(jnp.bfloat16)
    right_edge = (jax.nn.sigmoid(values[3]) * values[2]).astype(jnp.bfloat16)
    return (left_edge, right_edge)

def tail_grads(product_rows, gate_pre, cotangent_rows, output_weight):
    prod_normed, prod_inverse = layer_stats(product_rows.astype(jnp.float32), 0)
    weights = output_weight.astype(jnp.float32)
    update_pre = jnp.einsum('hrk,hd->rkd', rounded(prod_normed), weights)
    gate_open = jax.nn.sigmoid(gate_pre)
    incoming = cotangent_rows.astype(jnp.float32)
    grad_gate = (incoming * update_pre * gate_open * (1.0 - gate_open)).astype(jnp.bfloat16)
    grad_update = rounded(incoming * gate_open)
    grad_normed = jnp.einsum('rkd,hd->hrk', grad_update, weights)
    grad_product = layer_backward(grad_normed, prod_normed, prod_inverse, 0).astype(jnp.bfloat16)
    return (grad_product, grad_gate)

def reference(pair_state, cotangent, atom_feats, atom_token, window_count, input_weight, output_weight, atom_weight, left_weight, right_weight):
    live_slot = jnp.arange(ATOMS) % WIN < jnp.repeat(window_count, WIN)
    live_float = live_slot.astype(jnp.float32)
    atom_pre = jnp.dot(atom_feats, atom_weight, preferred_element_type=jnp.float32)
    atom_hidden = jax.nn.silu(atom_pre).astype(jnp.bfloat16)
    token_sum = jax.ops.segment_sum(atom_hidden.astype(jnp.float32) * live_float[:, None], atom_token, num_segments=N)
    token_count = jax.ops.segment_sum(live_float, atom_token, num_segments=N)
    single = (token_sum / token_count[:, None]).astype(jnp.bfloat16)
    left_bias = jnp.dot(single, left_weight, preferred_element_type=jnp.float32).astype(jnp.bfloat16)
    right_bias = jnp.dot(single, right_weight, preferred_element_type=jnp.float32).astype(jnp.bfloat16)
    pair_blocks = pair_state.reshape(N_PAIR, ROWS, N, C)
    cotangent_blocks = cotangent.reshape(N_PAIR, ROWS, N, C)
    left_blocks = left_bias.reshape(N_PAIR, ROWS, C)

    def front_edges(operands):
        normed, inverse, values, gate_pre = pair_front(operands[0], operands[1], right_bias, input_weight)
        return edge_values(values)
    left_edge, right_edge = lax.map(front_edges, (pair_blocks, left_blocks))
    left_edge = left_edge.transpose(1, 0, 2, 3).reshape(CH, N, N)
    right_edge = right_edge.transpose(1, 0, 2, 3).reshape(CH, N, N)

    def triangle(operands):
        return jnp.dot(operands[0].astype(jnp.float32), operands[1].astype(jnp.float32).T, precision=HIGHEST).astype(jnp.bfloat16)
    product = lax.map(triangle, (left_edge, right_edge))
    product_blocks = product.reshape(CH, N_PAIR, ROWS, N).transpose(1, 0, 2, 3)

    def tail_step(operands):
        pair_rows, left_rows, product_rows, cotangent_rows = operands
        normed, inverse, values, gate_pre = pair_front(pair_rows, left_rows, right_bias, input_weight)
        return tail_grads(product_rows, gate_pre, cotangent_rows, output_weight)
    grad_product, grad_gate = lax.map(tail_step, (pair_blocks, left_blocks, product_blocks, cotangent_blocks))
    grad_product = grad_product.transpose(1, 0, 2, 3).reshape(CH, N, N)

    def edge_grads(operands):
        grad_float = operands[0].astype(jnp.float32)
        left_grad = jnp.dot(grad_float, operands[2].astype(jnp.float32), precision=HIGHEST).astype(jnp.bfloat16)
        right_grad = jnp.dot(grad_float.T, operands[1].astype(jnp.float32), precision=HIGHEST).astype(jnp.bfloat16)
        return (left_grad, right_grad)
    left_grad, right_grad = lax.map(edge_grads, (grad_product, left_edge, right_edge))
    left_grad = left_grad.reshape(CH, N_PAIR, ROWS, N).transpose(1, 0, 2, 3)
    right_grad = right_grad.reshape(CH, N_PAIR, ROWS, N).transpose(1, 0, 2, 3)

    def final_step(operands):
        pair_rows, left_rows, left_flow, right_flow, gate_rows = operands
        normed, inverse, values, gate_pre = pair_front(pair_rows, left_rows, right_bias, input_weight)
        left_flow = left_flow.astype(jnp.float32)
        right_flow = right_flow.astype(jnp.float32)
        left_sigmoid = jax.nn.sigmoid(values[1])
        right_sigmoid = jax.nn.sigmoid(values[3])
        branch_grads = [rounded(left_flow * left_sigmoid), rounded(left_flow * values[0] * left_sigmoid * (1.0 - left_sigmoid)), rounded(right_flow * right_sigmoid), rounded(right_flow * values[2] * right_sigmoid * (1.0 - right_sigmoid))]
        weights = input_weight.astype(jnp.float32)
        grad_hidden = jnp.einsum('rkd,cd->rkc', gate_rows.astype(jnp.float32), weights[:, 4 * CH:])
        for quarter in range(4):
            grad_hidden = grad_hidden + jnp.einsum('hrk,ch->rkc', branch_grads[quarter], weights[:, quarter * CH:(quarter + 1) * CH])
        grad_inputs = layer_backward(grad_hidden, normed, inverse, -1)
        return (grad_inputs.astype(jnp.bfloat16), lax.optimization_barrier(jnp.sum(grad_inputs, axis=1)), lax.optimization_barrier(jnp.sum(grad_inputs, axis=0)))
    pair_grad, left_total, right_parts = lax.map(final_step, (pair_blocks, left_blocks, left_grad, right_grad, grad_gate))
    pair_grad = pair_grad.reshape(N, N, C)
    left_total = left_total.reshape(N, C)
    right_total = lax.optimization_barrier(jnp.sum(right_parts, axis=0))
    single_grad = (jnp.dot(left_total, left_weight.astype(jnp.float32).T, precision=HIGHEST) + jnp.dot(right_total, right_weight.astype(jnp.float32).T, precision=HIGHEST)).astype(jnp.bfloat16)
    picked = single_grad.astype(jnp.float32)[atom_token] / token_count[atom_token][:, None]
    hidden_grad = jnp.where(live_slot[:, None], picked, jnp.float32(0.0))
    atom_sigmoid = jax.nn.sigmoid(atom_pre)
    pre_grad = (hidden_grad * atom_sigmoid * (1.0 + atom_pre * (1.0 - atom_sigmoid))).astype(jnp.bfloat16)
    atom_grad = jnp.dot(pre_grad, atom_weight.T, preferred_element_type=jnp.float32).astype(jnp.bfloat16)
    return (pair_grad, atom_grad)
```

```python
import jax
import jax.numpy as jnp
from jax import lax
from jax.experimental import pallas as pl
from jax.experimental.pallas import tpu as pltpu
from jax.sharding import PartitionSpec as P

EPSILON = 1e-05
F32 = jnp.float32
BF16 = jnp.bfloat16
ROWS = 16
COLS = 128
CH = 128
DEV = 128
TOK = 512
WIN = 32
PAIR_DEV = 32
ATOM_DEV = 4
CHUNK = 32


def dot_nn(a, b):
    return lax.dot_general(a, b, (((1,), (0,)), ((), ())), preferred_element_type=F32)


def dot_nt(a, b):
    return lax.dot_general(a, b, (((1,), (1,)), ((), ())), preferred_element_type=F32)


def dot_tn(a, b):
    return lax.dot_general(a, b, (((0,), (0,)), ((), ())), preferred_element_type=F32)


def split(x):
    high = x.astype(BF16)
    return high, (x - high.astype(F32)).astype(BF16)


def sigmoid(x):
    return 0.5 * jnp.tanh(0.5 * x) + 0.5


def loop(start, stop, step):
    def run(i, carry):
        step(i)
        return carry

    lax.fori_loop(start, stop, run, 0)


def kernel(
    pair_ref,
    cot_ref,
    feat_ref,
    tok_ref,
    count_ref,
    iw_ref,
    ow_ref,
    aw_ref,
    lw_ref,
    rw_ref,
    pg_ref,
    ag_ref,
    member_ref,
    dsilu_ref,
    bias_msg,
    right_in,
    left_in,
    right_bias,
    right_inv,
    left_bias,
    left_inv,
    wt_ref,
    wt5_ref,
    mt_ref,
    normed_ref,
    inv_ref,
    hidden_ref,
    sig_left,
    sig_right,
    der_left,
    der_right,
    gate_ref,
    gn_ref,
    gg_ref,
    work_a,
    work_b,
    edge_out,
    edge_in,
    prod_out,
    prod_in,
    gp_out,
    gp_in,
    grad_out,
    grad_in,
    col_acc,
    row_ext,
    col_ext,
    row_msg,
    col_msg,
    row_in,
    col_in,
    send_sem,
    recv_sem,
):
    pos = lax.axis_index("pair")
    y = lax.axis_index("atom")
    me = pos * ATOM_DEV + y
    z = pos // 8
    x = (pos // 2) % 4
    c = pos % 2

    def remote(src, dst, sem, p, a):
        pltpu.make_async_remote_copy(
            src_ref=src,
            dst_ref=dst,
            send_sem=send_sem.at[sem],
            recv_sem=recv_sem.at[sem],
            device_id=(p, a),
            device_id_type=pl.DeviceIdType.MESH,
        ).start()

    def local(src, dst, sem):
        pltpu.make_async_copy(src, dst, recv_sem.at[sem]).start()

    def either(src, dst, sem, p, a, is_self):
        @pl.when(is_self)
        def _():
            local(src, dst, sem)

        @pl.when(jnp.logical_not(is_self))
        def _():
            remote(src, dst, sem, p, a)

    def wait_recv(ref, sem):
        pltpu.make_async_copy(ref, ref, recv_sem.at[sem]).wait()

    def wait_send(ref, sem):
        pltpu.make_async_copy(ref, ref, send_sem.at[sem]).wait()

    def plane(step):
        return (z + step) % 4

    def send_plane(step, zc, send_one, self_one):
        def one(q):
            p = zc * 8 + ((x + q // 8) % 4) * 2 + (c + q % 2) % 2
            a = (y + (q // 2) % 4) % 4
            send_one(p, a)

        if step == 0:
            self_one()
            loop(1, CHUNK, one)
        else:
            loop(0, CHUNK, one)

    atom_pre = dot_nn(feat_ref[...], aw_ref[...])
    atom_sig = sigmoid(atom_pre)
    atom_hidden = (atom_pre * atom_sig).astype(BF16)
    dsilu_ref[...] = atom_sig * (1.0 + atom_pre * (1.0 - atom_sig))
    slot = lax.broadcasted_iota(jnp.int32, (1, DEV), 1)
    live_count = jnp.full((1, DEV), 0, jnp.int32)
    for w in range(4):
        live_count = jnp.where(slot // WIN == w, count_ref[w], live_count)
    live = slot % WIN < live_count
    row8 = lax.broadcasted_iota(jnp.int32, (8, DEV), 0)
    lane8 = lax.broadcasted_iota(jnp.int32, (8, DEV), 1)
    member = jnp.where(
        (tok_ref[...] == me * 4 - 1 + row8) & (row8 < 5) & live, F32(1.0), F32(0.0)
    )
    member_ref[...] = member
    high, low = split(dot_nn(member.astype(BF16), atom_hidden))
    counts = jnp.sum(member, axis=1, keepdims=True)
    count_row = jnp.sum(jnp.where(lane8 == row8, counts, 0.0), axis=0, keepdims=True)
    for n, w_ref in enumerate((lw_ref, rw_ref)):
        weight = w_ref[...]
        sums = dot_nn(high, weight) + dot_nn(low, weight)
        bias_msg[n] = jnp.where(row8 == 5, count_row, sums)

    block = me // PAIR_DEV
    place = me % PAIR_DEV
    right_src = bias_msg.at[1]
    right_dst = right_in.at[pl.ds(pl.multiple_of(place * 8, 8), 8)]
    right_self = block == y
    either(right_src, right_dst, 0, pos, block, right_self)
    loop(1, PAIR_DEV, lambda q: remote(right_src, right_dst, 0, (pos + q) % PAIR_DEV, block))
    right_lead = (place == 0) & (me > 0)
    right_lead_self = right_lead & (block - 1 == y)

    @pl.when(right_lead)
    def _():
        lead_dst = right_in.at[pl.ds(PAIR_DEV * 8, 8)]
        either(right_src, lead_dst, 1, pos, block - 1, block - 1 == y)
        loop(
            1, PAIR_DEV, lambda q: remote(right_src, lead_dst, 1, (pos + q) % PAIR_DEV, block - 1)
        )

    left_src = bias_msg.at[0]
    left_dst = left_in.at[pl.ds(pl.multiple_of(y * 8, 8), 8)]
    local(left_src, left_dst, 2)
    loop(1, ATOM_DEV, lambda q: remote(left_src, left_dst, 2, pos, (y + q) % ATOM_DEV))
    left_lead = (y == 0) & (pos > 0)

    @pl.when(left_lead)
    def _():
        loop(
            0,
            ATOM_DEV,
            lambda q: remote(
                left_src, left_in.at[pl.ds(ATOM_DEV * 8, 8)], 3, pos - 1, (y + q) % ATOM_DEV
            ),
        )

    for q in range(4):
        turned = iw_ref[:, q * CH : (q + 1) * CH].astype(F32).T.astype(BF16)
        for zc in range(4):
            wt_ref[zc, q * CHUNK : (q + 1) * CHUNK, :] = turned[zc * CHUNK : (zc + 1) * CHUNK, :]
    wt5_ref[...] = iw_ref[:, 4 * CH :].astype(F32).T.astype(BF16)
    mt_ref[...] = ow_ref[...].astype(F32).T.astype(BF16)

    @pl.when(y == ATOM_DEV - 1)
    def _():
        right_in[pl.ds(PAIR_DEV * 8, 8), :] = jnp.zeros((8, CH), F32)

    @pl.when(pos == PAIR_DEV - 1)
    def _():
        left_in[pl.ds(ATOM_DEV * 8, 8), :] = jnp.zeros((8, CH), F32)

    wait_recv(right_in.at[pl.ds(0, PAIR_DEV * 8)], 0)

    @pl.when(y < ATOM_DEV - 1)
    def _():
        wait_recv(right_in.at[pl.ds(PAIR_DEV * 8, 8)], 1)

    wait_recv(left_in.at[pl.ds(0, ATOM_DEV * 8)], 2)

    @pl.when(pos < PAIR_DEV - 1)
    def _():
        wait_recv(left_in.at[pl.ds(ATOM_DEV * 8, 8)], 3)

    def finish_bias(src, bias_ref, inverse_ref, n):
        lane = lax.broadcasted_iota(jnp.int32, (n, CH), 1)
        count_own = src[pl.ds(5, n, stride=8), :]
        count_next = src[pl.ds(13, n, stride=8), :]
        for q in range(4):
            total = src[pl.ds(1 + q, n, stride=8), :]
            number = jnp.where(lane == 1 + q, count_own, 0.0)
            if q == 3:
                total = total + src[pl.ds(8, n, stride=8), :]
                number = number + jnp.where(lane == 0, count_next, 0.0)
            inverse = 1.0 / jnp.sum(number, axis=1, keepdims=True)
            bias_ref[pl.ds(q, n, stride=4), :] = (total * inverse).astype(BF16).astype(F32)
            inverse_ref[pl.ds(q, n, stride=4), :] = jnp.broadcast_to(inverse, (n, CH))

    finish_bias(right_in, right_bias, right_inv, PAIR_DEV)
    finish_bias(left_in, left_bias, left_inv, ATOM_DEV)

    def front(r):
        values = pair_ref[r].astype(F32) + left_bias[pl.ds(r, 1), :] + right_bias[...]
        values = values.T
        centre = jnp.mean(values, axis=0, keepdims=True)
        shifted = values - centre
        inverse = lax.rsqrt(jnp.mean(shifted * shifted, axis=0, keepdims=True) + EPSILON)
        normed = shifted * inverse
        normed_ref[r] = normed
        inv_ref[pl.ds(r, 1), :] = inverse
        hidden_ref[r] = normed.astype(BF16)

    loop(0, ROWS, front)

    edge_dst = edge_in.at[:, y, pl.ds(pl.multiple_of(pos * ROWS, ROWS), ROWS)]
    for step in range(4):
        zc = plane(step)
        first = pl.multiple_of(zc * CHUNK, CHUNK)

        def edges(r):
            pre = dot_nn(wt_ref[zc], hidden_ref[r])
            left_sig = sigmoid(pre[CHUNK : 2 * CHUNK])
            right_sig = sigmoid(pre[3 * CHUNK :])
            left = left_sig * pre[:CHUNK]
            right = right_sig * pre[2 * CHUNK : 3 * CHUNK]
            work_a[pl.ds(r, CHUNK, stride=ROWS), :] = left
            work_b[pl.ds(r, CHUNK, stride=ROWS), :] = right
            sig_left[r, pl.ds(first, CHUNK), :] = left_sig
            sig_right[r, pl.ds(first, CHUNK), :] = right_sig
            der_left[r, pl.ds(first, CHUNK), :] = left * (1.0 - left_sig)
            der_right[r, pl.ds(first, CHUNK), :] = right * (1.0 - right_sig)

        loop(0, ROWS, edges)
        span = CHUNK * ROWS
        edge_out[0, pl.ds(first, CHUNK)] = (
            work_a[:span, :].reshape(CHUNK, ROWS, COLS).astype(BF16)
        )
        edge_out[1, pl.ds(first, CHUNK)] = (
            work_b[:span, :].reshape(CHUNK, ROWS, COLS).astype(BF16)
        )
        send_plane(
            step,
            zc,
            lambda p, a: remote(edge_out.at[:, p * 4 + a], edge_dst, 4, p, a),
            lambda: local(edge_out.at[:, me], edge_dst, 4),
        )

    def gate(r):
        opened = sigmoid(dot_nn(wt5_ref[...], hidden_ref[r]))
        gated = cot_ref[r].astype(F32).T * opened
        gate_ref[r] = gated * (1.0 - opened)
        gn_ref[pl.ds(r, CH, stride=ROWS), :] = dot_nn(ow_ref[...], gated.astype(BF16))

    loop(0, ROWS, gate)

    def total(i, acc):
        chunk = gn_ref[pl.ds(pl.multiple_of(i * 128, 128), 128), :].reshape(8, ROWS, COLS)
        return acc + jnp.sum(chunk, axis=0)

    zero = jnp.zeros((ROWS, COLS), F32)
    gn_mean = lax.fori_loop(0, 16, total, zero) * (1.0 / CH)

    wait_recv(edge_in, 4)

    prod_dst = prod_in.at[me]
    for step in range(4):
        zc = plane(step)
        first = pl.multiple_of(zc * 128, 128)
        product = dot_nt(edge_in[0, 0, pl.ds(first, 128), :], edge_in[1, 0])
        for a in range(1, 4):
            product = product + dot_nt(edge_in[0, a, pl.ds(first, 128), :], edge_in[1, a])
        for a in range(4):
            prod_out[a, pl.ds(first, 128), :] = product[:, a * 128 : (a + 1) * 128].astype(BF16)

        def block_of(ref, p, a):
            return ref.at[a, pl.ds(pl.multiple_of(p * ROWS, ROWS), ROWS)]

        send_plane(
            step,
            zc,
            lambda p, a: remote(block_of(prod_out, p, a), prod_dst, 5, p, a),
            lambda: local(block_of(prod_out, pos, y), prod_dst, 5),
        )
    wait_recv(prod_in, 5)

    def sum_prod(i, acc):
        return acc + jnp.sum(prod_in[pl.ds(i * 8, 8)].astype(F32), axis=0)

    prod_mean = lax.fori_loop(0, 16, sum_prod, zero) * (1.0 / CH)

    def sum_squares(i, carry):
        squares, cross = carry
        shifted = prod_in[pl.ds(i * 8, 8)].astype(F32) - prod_mean[None]
        upstream = gn_ref[pl.ds(pl.multiple_of(i * 128, 128), 128), :].reshape(8, ROWS, COLS)
        return (
            squares + jnp.sum(shifted * shifted, axis=0),
            cross + jnp.sum(upstream * shifted, axis=0),
        )

    squares, cross = lax.fori_loop(0, 16, sum_squares, (zero, zero))
    prod_inv = lax.rsqrt(squares * (1.0 / CH) + EPSILON)
    cross = cross * prod_inv * prod_inv * (1.0 / CH)

    gp_dst = gp_in.at[y, pl.ds(pl.multiple_of(pos * ROWS, ROWS), ROWS)]
    for step in range(4):
        zc = plane(step)

        def grads(i):
            at = zc * CHUNK + i * 8
            shifted = prod_in[pl.ds(at, 8)].astype(F32) - prod_mean[None]
            upstream = gn_ref[pl.ds(pl.multiple_of(at * ROWS, 128), 128), :]
            upstream = upstream.reshape(8, ROWS, COLS)
            grad = prod_inv[None] * (upstream - gn_mean[None] - shifted * cross[None])
            gp_out[pl.ds(at, 8)] = grad.astype(BF16)

        loop(0, 4, grads)
        send_plane(
            step,
            zc,
            lambda p, a: remote(gp_out.at[p * 4 + a], gp_dst, 6, p, a),
            lambda: local(gp_out.at[me], gp_dst, 6),
        )

    def lay_normed(i):
        shifted = (prod_in[pl.ds(i * 8, 8)].astype(F32) - prod_mean[None]) * prod_inv[None]
        work_a[pl.ds(pl.multiple_of(i * 128, 128), 128), :] = shifted.reshape(128, COLS)

    loop(0, 16, lay_normed)

    def gate_grad(r):
        normed = work_a[pl.ds(r, CH, stride=ROWS), :].astype(BF16)
        gg_ref[r] = (dot_nn(mt_ref[...], normed) * gate_ref[r]).astype(BF16)

    loop(0, ROWS, gate_grad)

    wait_recv(gp_in, 6)

    for side in range(2):
        grad_dst = grad_in.at[side, me]
        for step in range(4):
            zc = plane(step)
            first = pl.multiple_of(zc * 128, 128)
            if side == 0:
                lhs = jnp.concatenate([gp_in[a, pl.ds(first, 128), :] for a in range(4)], axis=1)
            else:
                lhs = gp_in[zc].T
            for a in range(4):
                grad_out[side, a, pl.ds(first, 128), :] = dot_nn(
                    lhs, edge_in[1 - side, a]
                ).astype(BF16)

            def grad_block(p, a):
                return grad_out.at[side, a, pl.ds(pl.multiple_of(p * ROWS, ROWS), ROWS)]

            send_plane(
                step,
                zc,
                lambda p, a: remote(grad_block(p, a), grad_dst, 7 + side, p, a),
                lambda: local(grad_block(pos, y), grad_dst, 7 + side),
            )

    row_ext[...] = jnp.zeros_like(row_ext)
    col_ext[...] = jnp.zeros_like(col_ext)
    col_acc[...] = jnp.zeros_like(col_acc)

    for side, work in ((0, work_a), (1, work_b)):
        wait_recv(grad_in.at[side], 7 + side)

        def lay_grads(i):
            work[pl.ds(pl.multiple_of(i * 128, 128), 128), :] = (
                grad_in[side, pl.ds(i * 8, 8)].astype(F32).reshape(128, COLS)
            )

        loop(0, 16, lay_grads)

    def last(r):
        left = work_a[pl.ds(r, CH, stride=ROWS), :]
        right = work_b[pl.ds(r, CH, stride=ROWS), :]
        branches = jnp.concatenate(
            [
                (left * sig_left[r]).astype(BF16),
                (left * der_left[r]).astype(BF16),
                (right * sig_right[r]).astype(BF16),
                (right * der_right[r]).astype(BF16),
                gg_ref[r],
            ],
            axis=0,
        )
        grad = dot_nn(iw_ref[...], branches)
        normed = normed_ref[r]
        first_mean = jnp.mean(grad, axis=0, keepdims=True)
        cross_mean = jnp.mean(grad * normed, axis=0, keepdims=True)
        grad = inv_ref[pl.ds(r, 1), :] * (grad - first_mean - normed * cross_mean)
        grad = grad.T
        pg_ref[r] = grad.astype(BF16)
        col_acc[...] += grad
        row_ext[pl.ds(8 + r, 1), :] = jnp.sum(grad, axis=0, keepdims=True)

    loop(0, ROWS, last)

    row_ext[8:24, :] = row_ext[8:24, :] * left_inv[...]
    col_ext[8:136, :] = col_acc[...] * right_inv[...]
    for m in range(ATOM_DEV + 1):
        row_msg[m] = row_ext[7 + 4 * m : 15 + 4 * m, :]
    for m in range(PAIR_DEV + 1):
        col_msg[m] = col_ext[7 + 4 * m : 15 + 4 * m, :]

    local(row_msg.at[y], row_in.at[y], 9)

    def send_row(q):
        a = (y + q) % ATOM_DEV
        remote(row_msg.at[a], row_in.at[y], 9, pos, a)

    loop(1, ATOM_DEV, send_row)
    row_lead = pos < PAIR_DEV - 1

    @pl.when(row_lead)
    def _():
        remote(row_msg.at[ATOM_DEV], row_in.at[ATOM_DEV + y], 10, pos + 1, 0)

    def send_col(q):
        m = (place + q) % PAIR_DEV
        p = y * 8 + m // 4
        a = m % 4
        either(col_msg.at[m], col_in.at[pos], 11, p, a, (p == pos) & (a == y))

    loop(0, PAIR_DEV, send_col)
    col_lead = y < ATOM_DEV - 1
    col_lead_self = col_lead & (pos == (y + 1) * 8) & (y == 0)

    @pl.when(col_lead)
    def _():
        either(
            col_msg.at[PAIR_DEV],
            col_in.at[PAIR_DEV + pos],
            12,
            (y + 1) * 8,
            0,
            col_lead_self,
        )

    row_more = (y == 0) & (pos > 0)
    col_more = (place == 0) & (me > 0)

    @pl.when(jnp.logical_not(row_more))
    def _():
        row_in[ATOM_DEV:] = jnp.zeros((ATOM_DEV, 8, CH), F32)

    @pl.when(jnp.logical_not(col_more))
    def _():
        col_in[PAIR_DEV:] = jnp.zeros((PAIR_DEV, 8, CH), F32)

    wait_recv(row_in.at[pl.ds(0, ATOM_DEV)], 9)

    @pl.when(row_more)
    def _():
        wait_recv(row_in.at[pl.ds(ATOM_DEV, ATOM_DEV)], 10)

    wait_recv(col_in.at[pl.ds(0, PAIR_DEV)], 11)

    @pl.when(col_more)
    def _():
        wait_recv(col_in.at[pl.ds(PAIR_DEV, PAIR_DEV)], 12)

    single = jnp.zeros((8, 3 * CH), F32)
    for ref, w_ref in ((row_in, lw_ref), (col_in, rw_ref)):
        weight = w_ref[...]
        for part in split(jnp.sum(ref[...], axis=0)):
            single = single + dot_nt(part, weight)
    picked = dot_tn(member_ref[...].astype(BF16), single.astype(BF16))
    atom_grad = (picked * dsilu_ref[...]).astype(BF16)
    ag_ref[...] = dot_nt(atom_grad, aw_ref[...]).astype(BF16)

    wait_send(right_in.at[pl.ds(0, (PAIR_DEV - 1) * 8)], 0)

    @pl.when(jnp.logical_not(right_self))
    def _():
        wait_send(right_in.at[pl.ds(0, 8)], 0)

    @pl.when(right_lead)
    def _():
        wait_send(right_in.at[pl.ds(0, (PAIR_DEV - 1) * 8)], 1)

        @pl.when(jnp.logical_not(right_lead_self))
        def _():
            wait_send(right_in.at[pl.ds(0, 8)], 1)

    wait_send(left_in.at[pl.ds(0, (ATOM_DEV - 1) * 8)], 2)

    @pl.when(left_lead)
    def _():
        wait_send(left_in.at[pl.ds(0, ATOM_DEV * 8)], 3)

    wait_send(edge_out.at[:, pl.ds(0, DEV - 1)], 4)
    wait_send(prod_in.at[pl.ds(0, DEV - 1)], 5)
    wait_send(gp_out.at[pl.ds(0, DEV - 1)], 6)
    for side in range(2):
        wait_send(grad_in.at[side, pl.ds(0, DEV - 1)], 7 + side)
    wait_send(row_msg.at[pl.ds(0, ATOM_DEV - 1)], 9)

    @pl.when(row_lead)
    def _():
        wait_send(row_msg.at[pl.ds(0, 1)], 10)

    wait_send(col_msg.at[pl.ds(0, PAIR_DEV - 1)], 11)

    @pl.when(block != y)
    def _():
        wait_send(col_msg.at[pl.ds(0, 1)], 11)

    @pl.when(col_lead & jnp.logical_not(col_lead_self))
    def _():
        wait_send(col_msg.at[pl.ds(0, 1)], 12)


def body(
    pair_state,
    cotangent,
    atom_feats,
    atom_token,
    window_count,
    input_weight,
    output_weight,
    atom_weight,
    left_weight,
    right_weight,
):
    vmem = pl.BlockSpec(memory_space=pltpu.VMEM)
    rows = (ROWS, CH, COLS)
    scratch = [
        ((8, DEV), F32),
        ((DEV, 3 * CH), F32),
        ((2, 8, CH), F32),
        (((PAIR_DEV + 1) * 8 + 8, CH), F32),
        (((ATOM_DEV + 1) * 8 + 8, CH), F32),
        ((COLS, CH), F32),
        ((COLS, CH), F32),
        ((ROWS, CH), F32),
        ((ROWS, CH), F32),
        ((4, 4 * CHUNK, CH), BF16),
        ((CH, CH), BF16),
        ((CH, CH), BF16),
        (rows, F32),
        ((ROWS, COLS), F32),
        (rows, BF16),
        (rows, F32),
        (rows, F32),
        (rows, F32),
        (rows, F32),
        (rows, F32),
        ((CH * ROWS, COLS), F32),
        (rows, BF16),
        ((CH * ROWS, COLS), F32),
        ((CH * ROWS, COLS), F32),
        ((2, DEV, ROWS, COLS), BF16),
        ((2, 4, TOK, COLS), BF16),
        ((4, TOK, COLS), BF16),
        ((DEV, ROWS, COLS), BF16),
        ((DEV, ROWS, COLS), BF16),
        ((4, TOK, COLS), BF16),
        ((2, 4, TOK, COLS), BF16),
        ((2, DEV, ROWS, COLS), BF16),
        ((COLS, CH), F32),
        ((40, CH), F32),
        ((152, CH), F32),
        ((ATOM_DEV + 1, 8, CH), F32),
        ((PAIR_DEV + 1, 8, CH), F32),
        ((2 * ATOM_DEV, 8, CH), F32),
        ((2 * PAIR_DEV, 8, CH), F32),
    ]
    return pl.pallas_call(
        kernel,
        out_shape=(
            jax.ShapeDtypeStruct(pair_state.shape, BF16),
            jax.ShapeDtypeStruct(atom_feats.shape, BF16),
        ),
        in_specs=[
            vmem,
            vmem,
            vmem,
            vmem,
            pl.BlockSpec(memory_space=pltpu.SMEM),
            vmem,
            vmem,
            vmem,
            vmem,
            vmem,
        ],
        out_specs=(vmem, vmem),
        scratch_shapes=[pltpu.VMEM(shape, dtype) for shape, dtype in scratch]
        + [pltpu.SemaphoreType.DMA((13,)), pltpu.SemaphoreType.DMA((13,))],
        compiler_params=pltpu.CompilerParams(
            has_side_effects=True, vmem_limit_bytes=48 * 2**20
        ),
        cost_estimate=pl.CostEstimate(
            flops=1_700_000_000, bytes_accessed=2**21, transcendentals=2**20
        ),
    )(
        pair_state,
        cotangent,
        atom_feats,
        atom_token.reshape(1, -1),
        window_count,
        input_weight,
        output_weight,
        atom_weight,
        left_weight,
        right_weight,
    )


def solution(mesh):
    placed = (
        P("pair", "atom", None),
        P("pair", "atom", None),
        P(("pair", "atom"), None),
        P(("pair", "atom")),
        P(("pair", "atom")),
        P(),
        P(),
        P(),
        P(),
        P(),
    )
    return jax.shard_map(
        body,
        mesh=mesh,
        in_specs=placed,
        out_specs=(P("pair", "atom", None), P(("pair", "atom"), None)),
        check_vma=False,
    )
```

```python
import jax
import jax.numpy as jnp
from jax import lax
from jax.experimental import pallas as pl
from jax.experimental.pallas import tpu as pltpu
from jax.sharding import PartitionSpec as P

EPSILON = 1e-05
F32 = jnp.float32
BF16 = jnp.bfloat16
ROWS = 16
COLS = 128
CH = 128
DEV = 128
TOK = 512
WIN = 32
PAIR_DEV = 32
ATOM_DEV = 4
CHUNK = 32
UNROLL = 4

def dot_nn(a, b):
    return lax.dot_general(a, b, (((1,), (0,)), ((), ())), preferred_element_type=F32)

def dot_nt(a, b):
    return lax.dot_general(a, b, (((1,), (1,)), ((), ())), preferred_element_type=F32)

def dot_tn(a, b):
    return lax.dot_general(a, b, (((0,), (0,)), ((), ())), preferred_element_type=F32)

def split(x):
    high = x.astype(BF16)
    return high, (x - high.astype(F32)).astype(BF16)

def sigmoid(x):
    return 0.5 * jnp.tanh(0.5 * x) + 0.5

def loop(start, stop, step, unroll=1):
    def run(i, carry):
        step(i)
        return carry

    lax.fori_loop(start, stop, run, 0, unroll=unroll)

def kernel(
    pair_hbm,
    cot_hbm,
    feat_hbm,
    tok_hbm,
    count_ref,
    iw_hbm,
    ow_hbm,
    aw_hbm,
    lw_hbm,
    rw_hbm,
    pg_ref,
    ag_ref,
    pair_ref,
    cot_ref,
    feat_ref,
    tok_ref,
    iw_ref,
    ow_ref,
    aw_ref,
    lw_ref,
    rw_ref,
    member_ref,
    dsilu_ref,
    bias_msg,
    right_in,
    left_in,
    right_bias,
    right_inv,
    left_bias,
    left_inv,
    wt_ref,
    wt5_ref,
    mt_ref,
    normed_ref,
    inv_ref,
    hidden_ref,
    sig_left,
    sig_right,
    der_left,
    der_right,
    gate_ref,
    gn_ref,
    gg_ref,
    work_a,
    work_b,
    edge_out,
    edge_in,
    prod_out,
    prod_in,
    gp_out,
    gp_in,
    grad_out,
    grad_in,
    col_acc,
    row_ext,
    col_ext,
    row_msg,
    col_msg,
    row_in,
    col_in,
    send_sem,
    recv_sem,
    load_sem,
):
    pos = lax.axis_index("pair")
    y = lax.axis_index("atom")
    me = pos * ATOM_DEV + y
    z = pos // 8
    x = (pos // 2) % 4
    c = pos % 2

    def remote(src, dst, sem, p, a):
        pltpu.make_async_remote_copy(
            src_ref=src,
            dst_ref=dst,
            send_sem=send_sem.at[sem],
            recv_sem=recv_sem.at[sem],
            device_id=(p, a),
            device_id_type=pl.DeviceIdType.MESH,
        ).start()

    def local(src, dst, sem):
        pltpu.make_async_copy(src, dst, recv_sem.at[sem]).start()

    def either(src, dst, sem, p, a, is_self):
        @pl.when(is_self)
        def _():
            local(src, dst, sem)

        @pl.when(jnp.logical_not(is_self))
        def _():
            remote(src, dst, sem, p, a)

    def wait_recv(ref, sem):
        pltpu.make_async_copy(ref, ref, recv_sem.at[sem]).wait()

    def wait_send(ref, sem):
        pltpu.make_async_copy(ref, ref, send_sem.at[sem]).wait()

    def channel(p, a):
        return ((p // 8 + (p // 2) % 4 + a) % 4) * CHUNK + ((p // 2) % 4) * 8 + a * 2 + p % 2

    mine = channel(pos, y)
    group = (z + x + y) % 4

    def send_group(step, send_one, self_one):
        def one(q):
            xs = (x + q // 8) % 4
            a = (y + (q // 2) % 4) % 4
            p = ((group + step - xs - a + 8) % 4) * 8 + xs * 2 + (c + q % 2) % 2
            send_one(p, a)

        if step == 0:
            self_one()
            loop(1, CHUNK, one)
        else:
            loop(0, CHUNK, one)

    def plane(step):
        return (z + step) % 4

    def send_plane(step, zc, send_one, self_one):
        def one(q):
            p = zc * 8 + ((x + q // 8) % 4) * 2 + (c + q % 2) % 2
            a = (y + (q // 2) % 4) % 4
            send_one(p, a)

        if step == 0:
            self_one()
            loop(1, CHUNK, one)
        else:
            loop(0, CHUNK, one)

    barrier = pltpu.get_barrier_semaphore()

    def greet(q):
        to = (me + q) % DEV
        pl.semaphore_signal(
            barrier,
            inc=1,
            device_id=(to // ATOM_DEV, to % ATOM_DEV),
            device_id_type=pl.DeviceIdType.MESH,
        )

    loop(1, DEV, greet)

    loads = [
        pltpu.make_async_copy(src, dst, load_sem.at[n])
        for n, (src, dst) in enumerate(
            (
                (feat_hbm, feat_ref),
                (aw_hbm, aw_ref),
                (tok_hbm, tok_ref),
                (lw_hbm, lw_ref),
                (rw_hbm, rw_ref),
                (iw_hbm, iw_ref),
                (ow_hbm, ow_ref),
                (pair_hbm, pair_ref),
                (cot_hbm, cot_ref),
            )
        )
    ]
    for load in loads:
        load.start()
    for load in loads[:5]:
        load.wait()

    atom_pre = dot_nn(feat_ref[...], aw_ref[...])
    atom_sig = sigmoid(atom_pre)
    atom_hidden = (atom_pre * atom_sig).astype(BF16)
    dsilu_ref[...] = atom_sig * (1.0 + atom_pre * (1.0 - atom_sig))
    slot = lax.broadcasted_iota(jnp.int32, (1, DEV), 1)
    live_count = jnp.full((1, DEV), 0, jnp.int32)
    for w in range(4):
        live_count = jnp.where(slot // WIN == w, count_ref[w], live_count)
    live = slot % WIN < live_count
    row8 = lax.broadcasted_iota(jnp.int32, (8, DEV), 0)
    lane8 = lax.broadcasted_iota(jnp.int32, (8, DEV), 1)
    member = jnp.where(
        (tok_ref[...] == me * 4 - 1 + row8) & (row8 < 5) & live, F32(1.0), F32(0.0)
    )
    member_ref[...] = member
    high, low = split(dot_nn(member.astype(BF16), atom_hidden))
    counts = jnp.sum(member, axis=1, keepdims=True)
    count_row = jnp.sum(jnp.where(lane8 == row8, counts, 0.0), axis=0, keepdims=True)
    for n, w_ref in enumerate((lw_ref, rw_ref)):
        weight = w_ref[...]
        sums = dot_nn(high, weight) + dot_nn(low, weight)
        bias_msg[n] = jnp.where(row8 == 5, count_row, sums)

    for load in loads[5:]:
        load.wait()
    for q in range(4):
        turned = iw_ref[:, q * CH : (q + 1) * CH].astype(F32).T.astype(BF16)
        for zc in range(4):
            wt_ref[zc, q * CHUNK : (q + 1) * CHUNK, :] = turned[zc * CHUNK : (zc + 1) * CHUNK, :]
    wt5_ref[...] = iw_ref[:, 4 * CH :].astype(F32).T.astype(BF16)
    mt_ref[...] = ow_ref[...].astype(F32).T.astype(BF16)

    pl.semaphore_wait(barrier, DEV - 1)

    block = me // PAIR_DEV
    place = me % PAIR_DEV
    right_src = bias_msg.at[1]
    right_dst = right_in.at[pl.ds(pl.multiple_of(place * 8, 8), 8)]
    right_self = block == y
    either(right_src, right_dst, 0, pos, block, right_self)
    loop(1, PAIR_DEV, lambda q: remote(right_src, right_dst, 0, (pos + q) % PAIR_DEV, block))
    right_lead = (place == 0) & (me > 0)
    right_lead_self = right_lead & (block - 1 == y)

    @pl.when(right_lead)
    def _():
        lead_dst = right_in.at[pl.ds(PAIR_DEV * 8, 8)]
        either(right_src, lead_dst, 1, pos, block - 1, block - 1 == y)
        loop(
            1, PAIR_DEV, lambda q: remote(right_src, lead_dst, 1, (pos + q) % PAIR_DEV, block - 1)
        )

    left_src = bias_msg.at[0]
    left_dst = left_in.at[pl.ds(pl.multiple_of(y * 8, 8), 8)]
    local(left_src, left_dst, 2)
    loop(1, ATOM_DEV, lambda q: remote(left_src, left_dst, 2, pos, (y + q) % ATOM_DEV))
    left_lead = (y == 0) & (pos > 0)

    @pl.when(left_lead)
    def _():
        loop(
            0,
            ATOM_DEV,
            lambda q: remote(
                left_src, left_in.at[pl.ds(ATOM_DEV * 8, 8)], 3, pos - 1, (y + q) % ATOM_DEV
            ),
        )

    @pl.when(y == ATOM_DEV - 1)
    def _():
        right_in[pl.ds(PAIR_DEV * 8, 8), :] = jnp.zeros((8, CH), F32)

    @pl.when(pos == PAIR_DEV - 1)
    def _():
        left_in[pl.ds(ATOM_DEV * 8, 8), :] = jnp.zeros((8, CH), F32)

    wait_recv(right_in.at[pl.ds(0, PAIR_DEV * 8)], 0)

    @pl.when(y < ATOM_DEV - 1)
    def _():
        wait_recv(right_in.at[pl.ds(PAIR_DEV * 8, 8)], 1)

    wait_recv(left_in.at[pl.ds(0, ATOM_DEV * 8)], 2)

    @pl.when(pos < PAIR_DEV - 1)
    def _():
        wait_recv(left_in.at[pl.ds(ATOM_DEV * 8, 8)], 3)

    def finish_bias(src, bias_ref, inverse_ref, n):
        lane = lax.broadcasted_iota(jnp.int32, (n, CH), 1)
        count_own = src[pl.ds(5, n, stride=8), :]
        count_next = src[pl.ds(13, n, stride=8), :]
        for q in range(4):
            total = src[pl.ds(1 + q, n, stride=8), :]
            number = jnp.where(lane == 1 + q, count_own, 0.0)
            if q == 3:
                total = total + src[pl.ds(8, n, stride=8), :]
                number = number + jnp.where(lane == 0, count_next, 0.0)
            inverse = 1.0 / jnp.sum(number, axis=1, keepdims=True)
            bias_ref[pl.ds(q, n, stride=4), :] = (total * inverse).astype(BF16).astype(F32)
            inverse_ref[pl.ds(q, n, stride=4), :] = jnp.broadcast_to(inverse, (n, CH))

    finish_bias(right_in, right_bias, right_inv, PAIR_DEV)
    finish_bias(left_in, left_bias, left_inv, ATOM_DEV)

    def front(r):
        values = pair_ref[r].astype(F32) + left_bias[pl.ds(r, 1), :] + right_bias[...]
        values = values.T
        centre = jnp.mean(values, axis=0, keepdims=True)
        shifted = values - centre
        inverse = lax.rsqrt(jnp.mean(shifted * shifted, axis=0, keepdims=True) + EPSILON)
        normed = shifted * inverse
        normed_ref[r] = normed
        inv_ref[pl.ds(r, 1), :] = inverse
        hidden_ref[r] = normed.astype(BF16)

    loop(0, ROWS, front, UNROLL)

    edge_dst = edge_in.at[:, y, pl.ds(pl.multiple_of(pos * ROWS, ROWS), ROWS)]
    for step in range(4):
        zc = (group + step) % 4
        first = pl.multiple_of(zc * CHUNK, CHUNK)

        def edges(r):
            pre = dot_nn(wt_ref[zc], hidden_ref[r])
            left_sig = sigmoid(pre[CHUNK : 2 * CHUNK])
            right_sig = sigmoid(pre[3 * CHUNK :])
            left = left_sig * pre[:CHUNK]
            right = right_sig * pre[2 * CHUNK : 3 * CHUNK]
            work_a[pl.ds(r, CHUNK, stride=ROWS), :] = left
            work_b[pl.ds(r, CHUNK, stride=ROWS), :] = right
            sig_left[r, pl.ds(first, CHUNK), :] = left_sig
            sig_right[r, pl.ds(first, CHUNK), :] = right_sig
            der_left[r, pl.ds(first, CHUNK), :] = left * (1.0 - left_sig)
            der_right[r, pl.ds(first, CHUNK), :] = right * (1.0 - right_sig)

        loop(0, ROWS, edges, UNROLL)
        span = CHUNK * ROWS
        edge_out[0, pl.ds(first, CHUNK)] = (
            work_a[:span, :].reshape(CHUNK, ROWS, COLS).astype(BF16)
        )
        edge_out[1, pl.ds(first, CHUNK)] = (
            work_b[:span, :].reshape(CHUNK, ROWS, COLS).astype(BF16)
        )
        send_group(
            step,
            lambda p, a: remote(edge_out.at[:, channel(p, a)], edge_dst, 4, p, a),
            lambda: local(edge_out.at[:, mine], edge_dst, 4),
        )

    def gate(r):
        opened = sigmoid(dot_nn(wt5_ref[...], hidden_ref[r]))
        gated = cot_ref[r].astype(F32).T * opened
        gate_ref[r] = gated * (1.0 - opened)
        gn_ref[pl.ds(r, CH, stride=ROWS), :] = dot_nn(ow_ref[...], gated.astype(BF16))

    loop(0, ROWS, gate, UNROLL)

    def total(i, acc):
        chunk = gn_ref[pl.ds(pl.multiple_of(i * 128, 128), 128), :].reshape(8, ROWS, COLS)
        return acc + jnp.sum(chunk, axis=0)

    zero = jnp.zeros((ROWS, COLS), F32)
    gn_mean = lax.fori_loop(0, 16, total, zero) * (1.0 / CH)

    wait_recv(edge_in, 4)

    prod_dst = prod_in.at[mine]
    for step in range(4):
        zc = plane(step)
        first = pl.multiple_of(zc * 128, 128)
        product = dot_nt(edge_in[0, 0, pl.ds(first, 128), :], edge_in[1, 0])
        for a in range(1, 4):
            product = product + dot_nt(edge_in[0, a, pl.ds(first, 128), :], edge_in[1, a])
        for a in range(4):
            prod_out[a, pl.ds(first, 128), :] = product[:, a * 128 : (a + 1) * 128].astype(BF16)

        def block_of(ref, p, a):
            return ref.at[a, pl.ds(pl.multiple_of(p * ROWS, ROWS), ROWS)]

        send_plane(
            step,
            zc,
            lambda p, a: remote(block_of(prod_out, p, a), prod_dst, 5, p, a),
            lambda: local(block_of(prod_out, pos, y), prod_dst, 5),
        )

    wait_recv(prod_in, 5)

    def sum_prod(i, acc):
        return acc + jnp.sum(prod_in[pl.ds(i * 8, 8)].astype(F32), axis=0)

    prod_mean = lax.fori_loop(0, 16, sum_prod, zero) * (1.0 / CH)

    def sum_squares(i, carry):
        squares, cross = carry
        shifted = prod_in[pl.ds(i * 8, 8)].astype(F32) - prod_mean[None]
        upstream = gn_ref[pl.ds(pl.multiple_of(i * 128, 128), 128), :].reshape(8, ROWS, COLS)
        return (
            squares + jnp.sum(shifted * shifted, axis=0),
            cross + jnp.sum(upstream * shifted, axis=0),
        )

    squares, cross = lax.fori_loop(0, 16, sum_squares, (zero, zero))
    prod_inv = lax.rsqrt(squares * (1.0 / CH) + EPSILON)
    cross = cross * prod_inv * prod_inv * (1.0 / CH)

    gp_dst = gp_in.at[y, pl.ds(pl.multiple_of(pos * ROWS, ROWS), ROWS)]
    for step in range(4):
        zc = (group + step) % 4

        def grads(i):
            at = zc * CHUNK + i * 8
            shifted = prod_in[pl.ds(at, 8)].astype(F32) - prod_mean[None]
            upstream = gn_ref[pl.ds(pl.multiple_of(at * ROWS, 128), 128), :]
            upstream = upstream.reshape(8, ROWS, COLS)
            grad = prod_inv[None] * (upstream - gn_mean[None] - shifted * cross[None])
            gp_out[pl.ds(at, 8)] = grad.astype(BF16)

        loop(0, 4, grads)
        send_group(
            step,
            lambda p, a: remote(gp_out.at[channel(p, a)], gp_dst, 6, p, a),
            lambda: local(gp_out.at[mine], gp_dst, 6),
        )

    def lay_normed(i):
        shifted = (prod_in[pl.ds(i * 8, 8)].astype(F32) - prod_mean[None]) * prod_inv[None]
        work_a[pl.ds(pl.multiple_of(i * 128, 128), 128), :] = shifted.reshape(128, COLS)

    loop(0, 16, lay_normed)

    def gate_grad(r):
        normed = work_a[pl.ds(r, CH, stride=ROWS), :].astype(BF16)
        gg_ref[r] = (dot_nn(mt_ref[...], normed) * gate_ref[r]).astype(BF16)

    loop(0, ROWS, gate_grad, UNROLL)

    wait_recv(gp_in, 6)

    for side in range(2):
        grad_dst = grad_in.at[side, mine]
        for step in range(4):
            zc = plane(step)
            first = pl.multiple_of(zc * 128, 128)
            if side == 0:
                lhs = jnp.concatenate([gp_in[a, pl.ds(first, 128), :] for a in range(4)], axis=1)
            else:
                lhs = gp_in[zc].T
            for a in range(4):
                grad_out[side, a, pl.ds(first, 128), :] = dot_nn(
                    lhs, edge_in[1 - side, a]
                ).astype(BF16)

            def grad_block(p, a):
                return grad_out.at[side, a, pl.ds(pl.multiple_of(p * ROWS, ROWS), ROWS)]

            send_plane(
                step,
                zc,
                lambda p, a: remote(grad_block(p, a), grad_dst, 7 + side, p, a),
                lambda: local(grad_block(pos, y), grad_dst, 7 + side),
            )

    row_ext[...] = jnp.zeros_like(row_ext)
    col_ext[...] = jnp.zeros_like(col_ext)
    col_acc[...] = jnp.zeros_like(col_acc)

    for side, work in ((0, work_a), (1, work_b)):
        wait_recv(grad_in.at[side], 7 + side)

        def lay_grads(i):
            work[pl.ds(pl.multiple_of(i * 128, 128), 128), :] = (
                grad_in[side, pl.ds(i * 8, 8)].astype(F32).reshape(128, COLS)
            )

        loop(0, 16, lay_grads)

    def last(r):
        left = work_a[pl.ds(r, CH, stride=ROWS), :]
        right = work_b[pl.ds(r, CH, stride=ROWS), :]
        branches = jnp.concatenate(
            [
                (left * sig_left[r]).astype(BF16),
                (left * der_left[r]).astype(BF16),
                (right * sig_right[r]).astype(BF16),
                (right * der_right[r]).astype(BF16),
                gg_ref[r],
            ],
            axis=0,
        )
        grad = dot_nn(iw_ref[...], branches)
        normed = normed_ref[r]
        first_mean = jnp.mean(grad, axis=0, keepdims=True)
        cross_mean = jnp.mean(grad * normed, axis=0, keepdims=True)
        grad = inv_ref[pl.ds(r, 1), :] * (grad - first_mean - normed * cross_mean)
        grad = grad.T
        pg_ref[r] = grad.astype(BF16)
        col_acc[...] += grad
        row_ext[pl.ds(8 + r, 1), :] = jnp.sum(grad, axis=0, keepdims=True)

    loop(0, ROWS, last, UNROLL)

    row_ext[8:24, :] = row_ext[8:24, :] * left_inv[...]
    col_ext[8:136, :] = col_acc[...] * right_inv[...]
    for m in range(ATOM_DEV + 1):
        row_msg[m] = row_ext[7 + 4 * m : 15 + 4 * m, :]
    for m in range(PAIR_DEV + 1):
        col_msg[m] = col_ext[7 + 4 * m : 15 + 4 * m, :]

    local(row_msg.at[y], row_in.at[y], 9)

    def send_row(q):
        a = (y + q) % ATOM_DEV
        remote(row_msg.at[a], row_in.at[y], 9, pos, a)

    loop(1, ATOM_DEV, send_row)
    row_lead = pos < PAIR_DEV - 1

    @pl.when(row_lead)
    def _():
        remote(row_msg.at[ATOM_DEV], row_in.at[ATOM_DEV + y], 10, pos + 1, 0)

    def send_col(q):
        m = (place + q) % PAIR_DEV
        p = y * 8 + m // 4
        a = m % 4
        either(col_msg.at[m], col_in.at[pos], 11, p, a, (p == pos) & (a == y))

    loop(0, PAIR_DEV, send_col)
    col_lead = y < ATOM_DEV - 1
    col_lead_self = col_lead & (pos == (y + 1) * 8) & (y == 0)

    @pl.when(col_lead)
    def _():
        either(
            col_msg.at[PAIR_DEV],
            col_in.at[PAIR_DEV + pos],
            12,
            (y + 1) * 8,
            0,
            col_lead_self,
        )

    row_more = (y == 0) & (pos > 0)
    col_more = (place == 0) & (me > 0)

    @pl.when(jnp.logical_not(row_more))
    def _():
        row_in[ATOM_DEV:] = jnp.zeros((ATOM_DEV, 8, CH), F32)

    @pl.when(jnp.logical_not(col_more))
    def _():
        col_in[PAIR_DEV:] = jnp.zeros((PAIR_DEV, 8, CH), F32)

    wait_recv(row_in.at[pl.ds(0, ATOM_DEV)], 9)

    @pl.when(row_more)
    def _():
        wait_recv(row_in.at[pl.ds(ATOM_DEV, ATOM_DEV)], 10)

    wait_recv(col_in.at[pl.ds(0, PAIR_DEV)], 11)

    @pl.when(col_more)
    def _():
        wait_recv(col_in.at[pl.ds(PAIR_DEV, PAIR_DEV)], 12)

    single = jnp.zeros((8, 3 * CH), F32)
    for ref, w_ref in ((row_in, lw_ref), (col_in, rw_ref)):
        weight = w_ref[...]
        for part in split(jnp.sum(ref[...], axis=0)):
            single = single + dot_nt(part, weight)
    picked = dot_tn(member_ref[...].astype(BF16), single.astype(BF16))
    atom_grad = (picked * dsilu_ref[...]).astype(BF16)
    ag_ref[...] = dot_nt(atom_grad, aw_ref[...]).astype(BF16)

    wait_send(right_in.at[pl.ds(0, (PAIR_DEV - 1) * 8)], 0)

    @pl.when(jnp.logical_not(right_self))
    def _():
        wait_send(right_in.at[pl.ds(0, 8)], 0)

    @pl.when(right_lead)
    def _():
        wait_send(right_in.at[pl.ds(0, (PAIR_DEV - 1) * 8)], 1)

        @pl.when(jnp.logical_not(right_lead_self))
        def _():
            wait_send(right_in.at[pl.ds(0, 8)], 1)

    wait_send(left_in.at[pl.ds(0, (ATOM_DEV - 1) * 8)], 2)

    @pl.when(left_lead)
    def _():
        wait_send(left_in.at[pl.ds(0, ATOM_DEV * 8)], 3)

    wait_send(edge_out.at[:, pl.ds(0, DEV - 1)], 4)
    wait_send(prod_in.at[pl.ds(0, DEV - 1)], 5)
    wait_send(gp_out.at[pl.ds(0, DEV - 1)], 6)
    for side in range(2):
        wait_send(grad_in.at[side, pl.ds(0, DEV - 1)], 7 + side)
    wait_send(row_msg.at[pl.ds(0, ATOM_DEV - 1)], 9)

    @pl.when(row_lead)
    def _():
        wait_send(row_msg.at[pl.ds(0, 1)], 10)

    wait_send(col_msg.at[pl.ds(0, PAIR_DEV - 1)], 11)

    @pl.when(block != y)
    def _():
        wait_send(col_msg.at[pl.ds(0, 1)], 11)

    @pl.when(col_lead & jnp.logical_not(col_lead_self))
    def _():
        wait_send(col_msg.at[pl.ds(0, 1)], 12)

def body(
    pair_state,
    cotangent,
    atom_feats,
    atom_token,
    window_count,
    input_weight,
    output_weight,
    atom_weight,
    left_weight,
    right_weight,
):
    vmem = pl.BlockSpec(memory_space=pltpu.VMEM)
    hbm = pl.BlockSpec(memory_space=pl.ANY)
    rows = (ROWS, CH, COLS)
    scratch = [
        (rows, BF16),
        (rows, BF16),
        ((DEV, CH), BF16),
        ((1, DEV), jnp.int32),
        ((CH, 5 * CH), BF16),
        ((CH, CH), BF16),
        ((CH, 3 * CH), BF16),
        ((3 * CH, CH), BF16),
        ((3 * CH, CH), BF16),
        ((8, DEV), F32),
        ((DEV, 3 * CH), F32),
        ((2, 8, CH), F32),
        (((PAIR_DEV + 1) * 8 + 8, CH), F32),
        (((ATOM_DEV + 1) * 8 + 8, CH), F32),
        ((COLS, CH), F32),
        ((COLS, CH), F32),
        ((ROWS, CH), F32),
        ((ROWS, CH), F32),
        ((4, 4 * CHUNK, CH), BF16),
        ((CH, CH), BF16),
        ((CH, CH), BF16),
        (rows, F32),
        ((ROWS, COLS), F32),
        (rows, BF16),
        (rows, F32),
        (rows, F32),
        (rows, F32),
        (rows, F32),
        (rows, F32),
        ((CH * ROWS, COLS), F32),
        (rows, BF16),
        ((CH * ROWS, COLS), F32),
        ((CH * ROWS, COLS), F32),
        ((2, DEV, ROWS, COLS), BF16),
        ((2, 4, TOK, COLS), BF16),
        ((4, TOK, COLS), BF16),
        ((DEV, ROWS, COLS), BF16),
        ((DEV, ROWS, COLS), BF16),
        ((4, TOK, COLS), BF16),
        ((2, 4, TOK, COLS), BF16),
        ((2, DEV, ROWS, COLS), BF16),
        ((COLS, CH), F32),
        ((40, CH), F32),
        ((152, CH), F32),
        ((ATOM_DEV + 1, 8, CH), F32),
        ((PAIR_DEV + 1, 8, CH), F32),
        ((2 * ATOM_DEV, 8, CH), F32),
        ((2 * PAIR_DEV, 8, CH), F32),
    ]
    return pl.pallas_call(
        kernel,
        out_shape=(
            jax.ShapeDtypeStruct(pair_state.shape, BF16),
            jax.ShapeDtypeStruct(atom_feats.shape, BF16),
        ),
        in_specs=[hbm] * 4 + [pl.BlockSpec(memory_space=pltpu.SMEM)] + [hbm] * 5,
        out_specs=(vmem, vmem),
        scratch_shapes=[pltpu.VMEM(shape, dtype) for shape, dtype in scratch]
        + [pltpu.SemaphoreType.DMA((n,)) for n in (13, 13, 9)],
        compiler_params=pltpu.CompilerParams(
            collective_id=0, has_side_effects=True, vmem_limit_bytes=60 * 2**20
        ),
        cost_estimate=pl.CostEstimate(
            flops=1_700_000_000, bytes_accessed=2**21, transcendentals=2**20
        ),
    )(
        pair_state,
        cotangent,
        atom_feats,
        atom_token.reshape(1, -1),
        window_count,
        input_weight,
        output_weight,
        atom_weight,
        left_weight,
        right_weight,
    )

def solution(mesh):
    placed = (
        P("pair", "atom", None),
        P("pair", "atom", None),
        P(("pair", "atom"), None),
        P(("pair", "atom")),
        P(("pair", "atom")),
        P(),
        P(),
        P(),
        P(),
        P(),
    )
    return jax.shard_map(
        body,
        mesh=mesh,
        in_specs=placed,
        out_specs=(P("pair", "atom", None), P(("pair", "atom"), None)),
        check_vma=False,
    )
```

```python
import jax
import jax.numpy as jnp
from jax import lax
from jax.experimental import pallas as pl
from jax.experimental.pallas import tpu as pltpu
from jax.sharding import PartitionSpec as P

EPSILON = 1e-05
F32 = jnp.float32
BF16 = jnp.bfloat16
ROWS = 16
COLS = 128
CH = 128
DEV = 128
TOK = 512
WIN = 32
PAIR_DEV = 32
ATOM_DEV = 4
CHUNK = 32
UNROLL = 16
BIAS_ROWS = 6
SUM_ROWS = 5


def dot_nn(a, b):
    return lax.dot_general(a, b, (((1,), (0,)), ((), ())), preferred_element_type=F32)


def dot_nt(a, b):
    return lax.dot_general(a, b, (((1,), (1,)), ((), ())), preferred_element_type=F32)


def dot_tn(a, b):
    return lax.dot_general(a, b, (((0,), (0,)), ((), ())), preferred_element_type=F32)


def split(x):
    high = x.astype(BF16)
    return high, (x - high.astype(F32)).astype(BF16)


def sigmoid(x):
    return 0.5 * jnp.tanh(0.5 * x) + 0.5


def loop(start, stop, step, unroll=1):
    def run(i, carry):
        step(i)
        return carry

    lax.fori_loop(start, stop, run, 0, unroll=unroll)


def kernel(
    pair_hbm,
    cot_hbm,
    feat_hbm,
    tok_hbm,
    count_ref,
    iw_hbm,
    ow_hbm,
    aw_hbm,
    lw_hbm,
    rw_hbm,
    pg_hbm,
    ag_ref,
    pair_ref,
    cot_ref,
    feat_ref,
    tok_ref,
    iw_ref,
    ow_ref,
    aw_ref,
    lw_ref,
    rw_ref,
    member_ref,
    dsilu_ref,
    bias_msg,
    right_in,
    left_in,
    right_bias,
    right_inv,
    left_bias,
    left_inv,
    wt_ref,
    wt5_ref,
    mt_ref,
    normed_ref,
    inv_ref,
    hidden_ref,
    sig_left,
    sig_right,
    der_left,
    der_right,
    gate_ref,
    gn_ref,
    gg_ref,
    work_a,
    work_b,
    edge_out,
    edge_in,
    prod_out,
    prod_in,
    gp_out,
    gp_in,
    grad_out,
    grad_in,
    pg_ref,
    col_acc,
    row_ext,
    col_ext,
    row_msg,
    col_msg,
    row_in,
    col_in,
    send_sem,
    recv_sem,
    load_sem,
):
    pos = lax.axis_index("pair")
    y = lax.axis_index("atom")
    me = pos * ATOM_DEV + y
    z = pos // 8
    x = (pos // 2) % 4
    c = pos % 2

    def remote(src, dst, sem, p, a):
        pltpu.make_async_remote_copy(
            src_ref=src,
            dst_ref=dst,
            send_sem=send_sem.at[sem],
            recv_sem=recv_sem.at[sem],
            device_id=(p, a),
            device_id_type=pl.DeviceIdType.MESH,
        ).start()

    def local(src, dst, sem):
        pltpu.make_async_copy(src, dst, recv_sem.at[sem]).start()

    def either(src, dst, sem, p, a, is_self):
        @pl.when(is_self)
        def _():
            local(src, dst, sem)

        @pl.when(jnp.logical_not(is_self))
        def _():
            remote(src, dst, sem, p, a)

    def wait_recv(ref, sem):
        pltpu.make_async_copy(ref, ref, recv_sem.at[sem]).wait()

    def wait_send(ref, sem):
        pltpu.make_async_copy(ref, ref, send_sem.at[sem]).wait()

    def channel(p, a):
        return ((p // 8 + (p // 2) % 4) % 4) * CHUNK + ((p // 2) % 4) * 8 + a * 2 + p % 2

    mine = channel(pos, y)
    group = (z + x) % 4

    def send_group(step, send_one, self_one):
        def one(q):
            xs = (x + q // 8) % 4
            p = ((group + step + 4 - xs) % 4) * 8 + xs * 2 + (c + q % 2) % 2
            send_one(p, (y + (q // 2) % 4) % 4)

        if step % 4 == 0:
            self_one()
            loop(1, CHUNK, one)
        else:
            loop(0, CHUNK, one)

    def group_rows(zc):
        return [
            pl.ds(pl.multiple_of((((zc + 4 - xs) % 4) * 8 + xs * 2) * ROWS, 2 * ROWS), 2 * ROWS)
            for xs in range(4)
        ]

    barrier = pltpu.get_barrier_semaphore()

    def greet(q):
        to = (me + q) % DEV
        pl.semaphore_signal(
            barrier,
            inc=1,
            device_id=(to // ATOM_DEV, to % ATOM_DEV),
            device_id_type=pl.DeviceIdType.MESH,
        )

    loop(1, DEV, greet)

    loads = [
        pltpu.make_async_copy(src, dst, load_sem.at[n])
        for n, (src, dst) in enumerate(
            (
                (feat_hbm, feat_ref),
                (aw_hbm, aw_ref),
                (tok_hbm, tok_ref),
                (lw_hbm, lw_ref),
                (rw_hbm, rw_ref),
                (iw_hbm, iw_ref),
                (ow_hbm, ow_ref),
                (pair_hbm, pair_ref),
                (cot_hbm, cot_ref),
            )
        )
    ]
    for load in loads:
        load.start()
    for load in loads[:5]:
        load.wait()

    atom_pre = dot_nn(feat_ref[...], aw_ref[...])
    atom_sig = sigmoid(atom_pre)
    atom_hidden = (atom_pre * atom_sig).astype(BF16)
    dsilu_ref[...] = atom_sig * (1.0 + atom_pre * (1.0 - atom_sig))
    slot = lax.broadcasted_iota(jnp.int32, (1, DEV), 1)
    live_count = jnp.full((1, DEV), 0, jnp.int32)
    for w in range(4):
        live_count = jnp.where(slot // WIN == w, count_ref[w], live_count)
    live = slot % WIN < live_count
    row8 = lax.broadcasted_iota(jnp.int32, (8, DEV), 0)
    lane8 = lax.broadcasted_iota(jnp.int32, (8, DEV), 1)
    member = jnp.where(
        (tok_ref[...] == me * 4 - 1 + row8) & (row8 < 5) & live, F32(1.0), F32(0.0)
    )
    member_ref[...] = member
    high, low = split(dot_nn(member.astype(BF16), atom_hidden))
    counts = jnp.sum(member, axis=1, keepdims=True)
    count_row = jnp.sum(jnp.where(lane8 == row8, counts, 0.0), axis=0, keepdims=True)
    for n, w_ref in enumerate((lw_ref, rw_ref)):
        weight = w_ref[...]
        sums = dot_nn(high, weight) + dot_nn(low, weight)
        bias_msg[n] = jnp.where(row8 == 5, count_row, sums)

    for load in loads[5:]:
        load.wait()
    for q in range(4):
        turned = iw_ref[:, q * CH : (q + 1) * CH].astype(F32).T.astype(BF16)
        for zc in range(4):
            part = turned[zc * CHUNK : (zc + 1) * CHUNK, :]
            at = slice((q % 2) * CHUNK, (q % 2 + 1) * CHUNK)
            wt_ref[q // 2, zc, 0, at, :] = part
            wt_ref[q // 2, (zc + 3) % 4, 1, at, :] = part
    wt5_ref[...] = iw_ref[:, 4 * CH :].astype(F32).T.astype(BF16)
    mt_ref[...] = ow_ref[...].astype(F32).T.astype(BF16)


    pl.semaphore_wait(barrier, DEV - 1)

    block = me // PAIR_DEV
    place = me % PAIR_DEV
    right_src = bias_msg.at[1, pl.ds(0, BIAS_ROWS)]
    right_dst = right_in.at[pl.ds(pl.multiple_of(place * 8, 8), BIAS_ROWS)]
    right_self = block == y
    either(right_src, right_dst, 0, pos, block, right_self)
    loop(1, PAIR_DEV, lambda q: remote(right_src, right_dst, 0, (pos + q) % PAIR_DEV, block))
    right_lead = (place == 0) & (me > 0)
    right_lead_self = right_lead & (block - 1 == y)

    @pl.when(right_lead)
    def _():
        lead_dst = right_in.at[pl.ds(PAIR_DEV * 8, BIAS_ROWS)]
        either(right_src, lead_dst, 1, pos, block - 1, block - 1 == y)
        loop(
            1, PAIR_DEV, lambda q: remote(right_src, lead_dst, 1, (pos + q) % PAIR_DEV, block - 1)
        )

    left_src = bias_msg.at[0, pl.ds(0, BIAS_ROWS)]
    left_dst = left_in.at[pl.ds(pl.multiple_of(y * 8, 8), BIAS_ROWS)]
    local(left_src, left_dst, 2)
    loop(1, ATOM_DEV, lambda q: remote(left_src, left_dst, 2, pos, (y + q) % ATOM_DEV))
    left_lead = (y == 0) & (pos > 0)

    @pl.when(left_lead)
    def _():
        loop(
            0,
            ATOM_DEV,
            lambda q: remote(
                left_src,
                left_in.at[pl.ds(ATOM_DEV * 8, BIAS_ROWS)],
                3,
                pos - 1,
                (y + q) % ATOM_DEV,
            ),
        )

    @pl.when(y == ATOM_DEV - 1)
    def _():
        right_in[pl.ds(PAIR_DEV * 8, 8), :] = jnp.zeros((8, CH), F32)

    @pl.when(pos == PAIR_DEV - 1)
    def _():
        left_in[pl.ds(ATOM_DEV * 8, 8), :] = jnp.zeros((8, CH), F32)

    wait_recv(right_in.at[pl.ds(0, PAIR_DEV * BIAS_ROWS)], 0)

    @pl.when(y < ATOM_DEV - 1)
    def _():
        wait_recv(right_in.at[pl.ds(PAIR_DEV * 8, BIAS_ROWS)], 1)

    wait_recv(left_in.at[pl.ds(0, ATOM_DEV * BIAS_ROWS)], 2)

    @pl.when(pos < PAIR_DEV - 1)
    def _():
        wait_recv(left_in.at[pl.ds(ATOM_DEV * 8, BIAS_ROWS)], 3)


    def finish_bias(src, bias_ref, inverse_ref, n):
        lane = lax.broadcasted_iota(jnp.int32, (n, CH), 1)
        count_own = src[pl.ds(5, n, stride=8), :]
        count_next = src[pl.ds(13, n, stride=8), :]
        for q in range(4):
            total = src[pl.ds(1 + q, n, stride=8), :]
            number = jnp.where(lane == 1 + q, count_own, 0.0)
            if q == 3:
                total = total + src[pl.ds(8, n, stride=8), :]
                number = number + jnp.where(lane == 0, count_next, 0.0)
            inverse = 1.0 / jnp.sum(number, axis=1, keepdims=True)
            bias_ref[pl.ds(q, n, stride=4), :] = (total * inverse).astype(BF16).astype(F32)
            inverse_ref[pl.ds(q, n, stride=4), :] = jnp.broadcast_to(inverse, (n, CH))

    finish_bias(right_in, right_bias, right_inv, PAIR_DEV)
    finish_bias(left_in, left_bias, left_inv, ATOM_DEV)


    def front(r):
        values = pair_ref[r].astype(F32) + left_bias[pl.ds(r, 1), :] + right_bias[...]
        values = values.T
        centre = jnp.mean(values, axis=0, keepdims=True)
        shifted = values - centre
        inverse = lax.rsqrt(jnp.mean(shifted * shifted, axis=0, keepdims=True) + EPSILON)
        normed = shifted * inverse
        normed_ref[r] = normed
        inv_ref[pl.ds(r, 1), :] = inverse
        hidden_ref[r] = normed.astype(BF16)

    loop(0, ROWS, front, UNROLL)


    rows_here = pl.ds(pl.multiple_of(pos * ROWS, ROWS), ROWS)
    for side, sig_ref, der_ref, work in (
        (1, sig_right, der_right, work_b),
        (0, sig_left, der_left, work_a),
    ):
        edge_dst = edge_in.at[side, y, rows_here]
        for half in range(2):
            groups = [(group + 2 * half + n) % 4 for n in range(2)]
            firsts = [pl.multiple_of(zc * CHUNK, CHUNK) for zc in groups]

            def edges(r):
                weight = wt_ref[side, groups[0]].reshape(4 * CHUNK, CH)
                pre = dot_nn(weight, hidden_ref[r])
                for n in range(2):
                    value = pre[2 * n * CHUNK : (2 * n + 1) * CHUNK]
                    opened = sigmoid(pre[(2 * n + 1) * CHUNK : (2 * n + 2) * CHUNK])
                    edge = opened * value
                    work[pl.ds(n * CHUNK * ROWS + r, CHUNK, stride=ROWS), :] = edge
                    sig_ref[r, pl.ds(firsts[n], CHUNK), :] = opened
                    der_ref[r, pl.ds(firsts[n], CHUNK), :] = edge * (1.0 - opened)

            loop(0, ROWS, edges, UNROLL)
            for n in range(2):
                edge_out[side, pl.ds(firsts[n], CHUNK)] = (
                    work[n * CHUNK * ROWS : (n + 1) * CHUNK * ROWS, :]
                    .reshape(CHUNK, ROWS, COLS)
                    .astype(BF16)
                )
                step = 2 * half + n
                sem = 4 if side == 1 else 13 + step
                send_group(
                    step,
                    lambda p, a: remote(edge_out.at[side, channel(p, a)], edge_dst, sem, p, a),
                    lambda: local(edge_out.at[side, mine], edge_dst, sem),
                )

    def gate(r):
        opened = sigmoid(dot_nn(wt5_ref[...], hidden_ref[r]))
        gated = cot_ref[r].astype(F32).T * opened
        gate_ref[r] = gated * (1.0 - opened)
        gn_ref[pl.ds(r, CH, stride=ROWS), :] = dot_nn(ow_ref[...], gated.astype(BF16))

    loop(0, ROWS, gate, UNROLL)

    def total(i, acc):
        chunk = gn_ref[pl.ds(pl.multiple_of(i * 128, 128), 128), :].reshape(8, ROWS, COLS)
        return acc + jnp.sum(chunk, axis=0)

    zero = jnp.zeros((ROWS, COLS), F32)
    gn_mean = lax.fori_loop(0, 16, total, zero) * (1.0 / CH)


    prod_dst = prod_in.at[mine]

    def block_of(ref, p, a):
        return ref.at[a, pl.ds(pl.multiple_of(p * ROWS, ROWS), ROWS)]

    wait_recv(edge_in.at[1], 4)
    for step in range(4):
        wait_recv(edge_in.at[0, 0], 13 + step)
        rows = group_rows((group + 4 - step) % 4)
        product = None
        for a in range(4):
            lhs = jnp.concatenate([edge_in[0, a, run, :] for run in rows], axis=0)
            term = dot_nt(lhs, edge_in[1, a])
            product = term if product is None else product + term
        product = product.astype(BF16)
        for a in range(4):
            for n, run in enumerate(rows):
                prod_out[a, run, :] = product[
                    2 * ROWS * n : 2 * ROWS * (n + 1), COLS * a : COLS * (a + 1)
                ]
        send_group(
            (4 - step) % 4,
            lambda p, a: remote(block_of(prod_out, p, a), prod_dst, 5, p, a),
            lambda: local(block_of(prod_out, pos, y), prod_dst, 5),
        )
    wait_recv(prod_in, 5)

    def sum_prod(i, acc):
        return acc + jnp.sum(prod_in[pl.ds(i * 8, 8)].astype(F32), axis=0)

    prod_mean = lax.fori_loop(0, 16, sum_prod, zero) * (1.0 / CH)

    def sum_squares(i, carry):
        squares, cross = carry
        shifted = prod_in[pl.ds(i * 8, 8)].astype(F32) - prod_mean[None]
        upstream = gn_ref[pl.ds(pl.multiple_of(i * 128, 128), 128), :].reshape(8, ROWS, COLS)
        return (
            squares + jnp.sum(shifted * shifted, axis=0),
            cross + jnp.sum(upstream * shifted, axis=0),
        )

    squares, cross = lax.fori_loop(0, 16, sum_squares, (zero, zero))
    prod_inv = lax.rsqrt(squares * (1.0 / CH) + EPSILON)
    cross = cross * prod_inv * prod_inv * (1.0 / CH)


    gp_dst = gp_in.at[y, rows_here]
    for step in range(4):
        zc = (group + step) % 4

        def grads(i):
            at = zc * CHUNK + i * 8
            shifted = prod_in[pl.ds(at, 8)].astype(F32) - prod_mean[None]
            upstream = gn_ref[pl.ds(pl.multiple_of(at * ROWS, 128), 128), :]
            upstream = upstream.reshape(8, ROWS, COLS)
            grad = prod_inv[None] * (upstream - gn_mean[None] - shifted * cross[None])
            gp_out[pl.ds(at, 8)] = grad.astype(BF16)

        loop(0, 4, grads, 4)
        send_group(
            step,
            lambda p, a: remote(gp_out.at[channel(p, a)], gp_dst, 17 + step, p, a),
            lambda: local(gp_out.at[mine], gp_dst, 17 + step),
        )


    left_dst = grad_in.at[0, mine]
    for step in range(4):
        wait_recv(gp_in.at[0], 17 + step)
        rows = group_rows((group + 4 - step) % 4)
        lhs = jnp.concatenate(
            [jnp.concatenate([gp_in[a, run, :] for run in rows], axis=0) for a in range(4)], axis=1
        )
        for a in range(4):
            grad = dot_nn(lhs, edge_in[1, a]).astype(BF16)
            for n, run in enumerate(rows):
                grad_out[0, a, run, :] = grad[2 * ROWS * n : 2 * ROWS * (n + 1), :]
        send_group(
            (4 - step) % 4,
            lambda p, a: remote(block_of(grad_out.at[0], p, a), left_dst, 7, p, a),
            lambda: local(block_of(grad_out.at[0], pos, y), left_dst, 7),
        )
    for zc in range(4):
        lhs = gp_in[zc].T
        for a in range(4):
            grad_out[1, a, 128 * zc : 128 * (zc + 1), :] = dot_nn(lhs, edge_in[0, a]).astype(BF16)
    right_dst = grad_in.at[1, mine]
    for step in range(4):
        send_group(
            step,
            lambda p, a: remote(block_of(grad_out.at[1], p, a), right_dst, 8, p, a),
            lambda: local(block_of(grad_out.at[1], pos, y), right_dst, 8),
        )

    def lay_normed(i):
        shifted = (prod_in[pl.ds(i * 8, 8)].astype(F32) - prod_mean[None]) * prod_inv[None]
        work_a[pl.ds(pl.multiple_of(i * 128, 128), 128), :] = shifted.reshape(128, COLS)

    loop(0, 16, lay_normed, UNROLL)

    def gate_grad(r):
        normed = work_a[pl.ds(r, CH, stride=ROWS), :].astype(BF16)
        gg_ref[r] = (dot_nn(mt_ref[...], normed) * gate_ref[r]).astype(BF16)

    loop(0, ROWS, gate_grad, UNROLL)


    row_ext[...] = jnp.zeros_like(row_ext)
    col_ext[...] = jnp.zeros_like(col_ext)
    col_acc[...] = jnp.zeros_like(col_acc)

    def lay_grads(side, work):
        def lay(i):
            work[pl.ds(pl.multiple_of(i * 128, 128), 128), :] = (
                grad_in[side, pl.ds(i * 8, 8)].astype(F32).reshape(128, COLS)
            )

        loop(0, 16, lay, UNROLL)

    def branches(work, sig_ref, der_ref, r):
        flow = work[pl.ds(r, CH, stride=ROWS), :]
        return [(flow * sig_ref[r]).astype(BF16), (flow * der_ref[r]).astype(BF16)]

    def partial(r):
        left = branches(work_a, sig_left, der_left, r)
        gate_ref[r] = dot_nn(iw_ref[:, : 2 * CH], jnp.concatenate(left, axis=0)) + dot_nn(
            iw_ref[:, 4 * CH :], gg_ref[r]
        )

    wait_recv(grad_in.at[0], 7)
    lay_grads(0, work_a)
    loop(0, ROWS, partial, UNROLL)
    wait_recv(grad_in.at[1], 8)
    lay_grads(1, work_b)

    def last(r):
        right = branches(work_b, sig_right, der_right, r)
        grad = gate_ref[r] + dot_nn(iw_ref[:, 2 * CH : 4 * CH], jnp.concatenate(right, axis=0))
        normed = normed_ref[r]
        first_mean = jnp.mean(grad, axis=0, keepdims=True)
        cross_mean = jnp.mean(grad * normed, axis=0, keepdims=True)
        grad = inv_ref[pl.ds(r, 1), :] * (grad - first_mean - normed * cross_mean)
        grad = grad.T
        pg_ref[r] = grad.astype(BF16)
        col_acc[...] += grad
        row_ext[pl.ds(8 + r, 1), :] = jnp.sum(grad, axis=0, keepdims=True)

    loop(0, ROWS, last, UNROLL)


    store = pltpu.make_async_copy(pg_ref, pg_hbm, load_sem.at[9])
    store.start()

    row_ext[8:24, :] = row_ext[8:24, :] * left_inv[...]
    col_ext[8:136, :] = col_acc[...] * right_inv[...]
    for m in range(ATOM_DEV + 1):
        row_msg[m] = row_ext[7 + 4 * m : 15 + 4 * m, :]
    for m in range(PAIR_DEV + 1):
        col_msg[m] = col_ext[7 + 4 * m : 15 + 4 * m, :]

    used = pl.ds(0, SUM_ROWS)
    local(row_msg.at[y, used], row_in.at[y, used], 9)

    def send_row(q):
        a = (y + q) % ATOM_DEV
        remote(row_msg.at[a, used], row_in.at[y, used], 9, pos, a)

    loop(1, ATOM_DEV, send_row)
    row_lead = pos < PAIR_DEV - 1

    @pl.when(row_lead)
    def _():
        remote(row_msg.at[ATOM_DEV, used], row_in.at[ATOM_DEV + y, used], 10, pos + 1, 0)

    def send_col(q):
        m = (place + q) % PAIR_DEV
        p = y * 8 + m // 4
        a = m % 4
        either(col_msg.at[m, used], col_in.at[pos, used], 11, p, a, (p == pos) & (a == y))

    loop(0, PAIR_DEV, send_col)
    col_lead = y < ATOM_DEV - 1
    col_lead_self = col_lead & (pos == (y + 1) * 8) & (y == 0)

    @pl.when(col_lead)
    def _():
        either(
            col_msg.at[PAIR_DEV, used],
            col_in.at[PAIR_DEV + pos, used],
            12,
            (y + 1) * 8,
            0,
            col_lead_self,
        )

    row_more = (y == 0) & (pos > 0)
    col_more = (place == 0) & (me > 0)

    @pl.when(jnp.logical_not(row_more))
    def _():
        row_in[ATOM_DEV:] = jnp.zeros((ATOM_DEV, 8, CH), F32)

    @pl.when(jnp.logical_not(col_more))
    def _():
        col_in[PAIR_DEV:] = jnp.zeros((PAIR_DEV, 8, CH), F32)

    wait_recv(row_in.at[pl.ds(0, ATOM_DEV), used], 9)

    @pl.when(row_more)
    def _():
        wait_recv(row_in.at[pl.ds(ATOM_DEV, ATOM_DEV), used], 10)

    wait_recv(col_in.at[pl.ds(0, PAIR_DEV), used], 11)

    @pl.when(col_more)
    def _():
        wait_recv(col_in.at[pl.ds(PAIR_DEV, PAIR_DEV), used], 12)


    single = jnp.zeros((8, 3 * CH), F32)
    for ref, w_ref in ((row_in, lw_ref), (col_in, rw_ref)):
        weight = w_ref[...]
        sums = jnp.where(row8 < SUM_ROWS, jnp.sum(ref[...], axis=0), 0.0)
        for part in split(sums):
            single = single + dot_nt(part, weight)
    picked = dot_tn(member_ref[...].astype(BF16), single.astype(BF16))
    atom_grad = (picked * dsilu_ref[...]).astype(BF16)
    ag_ref[...] = dot_nt(atom_grad, aw_ref[...]).astype(BF16)

    store.wait()

    wait_send(right_in.at[pl.ds(0, (PAIR_DEV - 1) * BIAS_ROWS)], 0)

    @pl.when(jnp.logical_not(right_self))
    def _():
        wait_send(right_in.at[pl.ds(0, BIAS_ROWS)], 0)

    @pl.when(right_lead)
    def _():
        wait_send(right_in.at[pl.ds(0, (PAIR_DEV - 1) * BIAS_ROWS)], 1)

        @pl.when(jnp.logical_not(right_lead_self))
        def _():
            wait_send(right_in.at[pl.ds(0, BIAS_ROWS)], 1)

    wait_send(left_in.at[pl.ds(0, (ATOM_DEV - 1) * BIAS_ROWS)], 2)

    @pl.when(left_lead)
    def _():
        wait_send(left_in.at[pl.ds(0, ATOM_DEV * BIAS_ROWS)], 3)

    wait_send(edge_out.at[1, pl.ds(0, DEV - 1)], 4)
    for step in range(4):
        sent = pl.ds(0, CHUNK - 1 if step == 0 else CHUNK)
        wait_send(edge_out.at[0, sent], 13 + step)
        wait_send(gp_out.at[sent], 17 + step)
    wait_send(prod_in.at[pl.ds(0, DEV - 1)], 5)
    for side in range(2):
        wait_send(grad_in.at[side, pl.ds(0, DEV - 1)], 7 + side)
    wait_send(row_msg.at[pl.ds(0, ATOM_DEV - 1), used], 9)

    @pl.when(row_lead)
    def _():
        wait_send(row_msg.at[pl.ds(0, 1), used], 10)

    wait_send(col_msg.at[pl.ds(0, PAIR_DEV - 1), used], 11)

    @pl.when(block != y)
    def _():
        wait_send(col_msg.at[pl.ds(0, 1), used], 11)

    @pl.when(col_lead & jnp.logical_not(col_lead_self))
    def _():
        wait_send(col_msg.at[pl.ds(0, 1), used], 12)


def body(
    pair_state,
    cotangent,
    atom_feats,
    atom_token,
    window_count,
    input_weight,
    output_weight,
    atom_weight,
    left_weight,
    right_weight,
):
    vmem = pl.BlockSpec(memory_space=pltpu.VMEM)
    hbm = pl.BlockSpec(memory_space=pl.ANY)
    rows = (ROWS, CH, COLS)
    scratch = [
        (rows, BF16),
        (rows, BF16),
        ((DEV, CH), BF16),
        ((1, DEV), jnp.int32),
        ((CH, 5 * CH), BF16),
        ((CH, CH), BF16),
        ((CH, 3 * CH), BF16),
        ((3 * CH, CH), BF16),
        ((3 * CH, CH), BF16),
        ((8, DEV), F32),
        ((DEV, 3 * CH), F32),
        ((2, 8, CH), F32),
        (((PAIR_DEV + 1) * 8 + 8, CH), F32),
        (((ATOM_DEV + 1) * 8 + 8, CH), F32),
        ((COLS, CH), F32),
        ((COLS, CH), F32),
        ((ROWS, CH), F32),
        ((ROWS, CH), F32),
        ((2, 4, 2, 2 * CHUNK, CH), BF16),
        ((CH, CH), BF16),
        ((CH, CH), BF16),
        (rows, F32),
        ((ROWS, COLS), F32),
        (rows, BF16),
        (rows, F32),
        (rows, F32),
        (rows, F32),
        (rows, F32),
        (rows, F32),
        ((CH * ROWS, COLS), F32),
        (rows, BF16),
        ((CH * ROWS, COLS), F32),
        ((CH * ROWS, COLS), F32),
        ((2, DEV, ROWS, COLS), BF16),
        ((2, 4, TOK, COLS), BF16),
        ((4, TOK, COLS), BF16),
        ((DEV, ROWS, COLS), BF16),
        ((DEV, ROWS, COLS), BF16),
        ((4, TOK, COLS), BF16),
        ((2, 4, TOK, COLS), BF16),
        ((2, DEV, ROWS, COLS), BF16),
        (rows, BF16),
        ((COLS, CH), F32),
        ((40, CH), F32),
        ((152, CH), F32),
        ((ATOM_DEV + 1, 8, CH), F32),
        ((PAIR_DEV + 1, 8, CH), F32),
        ((2 * ATOM_DEV, 8, CH), F32),
        ((2 * PAIR_DEV, 8, CH), F32),
    ]
    return pl.pallas_call(
        kernel,
        out_shape=(
            jax.ShapeDtypeStruct(pair_state.shape, BF16),
            jax.ShapeDtypeStruct(atom_feats.shape, BF16),
        ),
        in_specs=[hbm] * 4 + [pl.BlockSpec(memory_space=pltpu.SMEM)] + [hbm] * 5,
        out_specs=(hbm, vmem),
        scratch_shapes=[pltpu.VMEM(shape, dtype) for shape, dtype in scratch]
        + [pltpu.SemaphoreType.DMA((n,)) for n in (21, 21, 10)],
        compiler_params=pltpu.CompilerParams(
            collective_id=0, has_side_effects=True, vmem_limit_bytes=60 * 2**20
        ),
        cost_estimate=pl.CostEstimate(
            flops=1_700_000_000, bytes_accessed=2**21, transcendentals=2**20
        ),
    )(
        pair_state,
        cotangent,
        atom_feats,
        atom_token.reshape(1, -1),
        window_count,
        input_weight,
        output_weight,
        atom_weight,
        left_weight,
        right_weight,
    )


def solution(mesh):
    placed = (
        P("pair", "atom", None),
        P("pair", "atom", None),
        P(("pair", "atom"), None),
        P(("pair", "atom")),
        P(("pair", "atom")),
        P(),
        P(),
        P(),
        P(),
        P(),
    )
    return jax.shard_map(
        body,
        mesh=mesh,
        in_specs=placed,
        out_specs=(P("pair", "atom", None), P(("pair", "atom"), None)),
        check_vma=False,
    )
```

```python
import jax
import jax.numpy as jnp
from jax import lax
from jax.experimental import pallas as pl
from jax.experimental.pallas import tpu as pltpu
from jax.sharding import PartitionSpec as P

EPSILON = 1e-05
F32 = jnp.float32
BF16 = jnp.bfloat16
ROWS = 16
COLS = 128
CH = 128
DEV = 128
TOK = 512
WIN = 32
PAIR_DEV = 32
ATOM_DEV = 4
CHUNK = 32
UNROLL = 16
BIAS_ROWS = 6
SUM_ROWS = 5


def dot_nn(a, b):
    return lax.dot_general(a, b, (((1,), (0,)), ((), ())), preferred_element_type=F32)


def dot_nt(a, b):
    return lax.dot_general(a, b, (((1,), (1,)), ((), ())), preferred_element_type=F32)


def dot_tn(a, b):
    return lax.dot_general(a, b, (((0,), (0,)), ((), ())), preferred_element_type=F32)


def split(x):
    high = x.astype(BF16)
    return high, (x - high.astype(F32)).astype(BF16)


def sigmoid(x):
    return 0.5 * jnp.tanh(0.5 * x) + 0.5


def loop(start, stop, step, unroll=1):
    def run(i, carry):
        step(i)
        return carry

    lax.fori_loop(start, stop, run, 0, unroll=unroll)


def kernel(
    pair_hbm,
    cot_hbm,
    feat_hbm,
    tok_hbm,
    count_ref,
    iw_hbm,
    ow_hbm,
    aw_hbm,
    lw_hbm,
    rw_hbm,
    pg_hbm,
    ag_ref,
    pair_ref,
    cot_ref,
    feat_ref,
    tok_ref,
    iw_ref,
    ow_ref,
    aw_ref,
    lw_ref,
    rw_ref,
    member_ref,
    dsilu_ref,
    bias_msg,
    right_in,
    left_in,
    right_bias,
    right_inv,
    left_bias,
    left_inv,
    wt_ref,
    wt5_ref,
    mt_ref,
    normed_ref,
    inv_ref,
    hidden_ref,
    sig_left,
    sig_right,
    der_left,
    der_right,
    gate_ref,
    gn_ref,
    gg_ref,
    work_a,
    work_b,
    edge_out,
    edge_in,
    prod_out,
    prod_in,
    gp_out,
    gp_in,
    grad_out,
    grad_in,
    pg_ref,
    col_acc,
    row_ext,
    col_ext,
    row_msg,
    col_msg,
    row_in,
    col_in,
    send_sem,
    recv_sem,
    load_sem,
):
    pos = lax.axis_index("pair")
    y = lax.axis_index("atom")
    me = pos * ATOM_DEV + y
    z = pos // 8
    x = (pos // 2) % 4
    c = pos % 2

    def remote(src, dst, sem, p, a):
        pltpu.make_async_remote_copy(
            src_ref=src,
            dst_ref=dst,
            send_sem=send_sem.at[sem],
            recv_sem=recv_sem.at[sem],
            device_id=(p, a),
            device_id_type=pl.DeviceIdType.MESH,
        ).start()

    def local(src, dst, sem):
        pltpu.make_async_copy(src, dst, recv_sem.at[sem]).start()

    def either(src, dst, sem, p, a, is_self):
        @pl.when(is_self)
        def _():
            local(src, dst, sem)

        @pl.when(jnp.logical_not(is_self))
        def _():
            remote(src, dst, sem, p, a)

    def wait_recv(ref, sem):
        pltpu.make_async_copy(ref, ref, recv_sem.at[sem]).wait()

    def wait_send(ref, sem):
        pltpu.make_async_copy(ref, ref, send_sem.at[sem]).wait()

    def channel(p, a):
        return ((p // 8 + (p // 2) % 4) % 4) * CHUNK + ((p // 2) % 4) * 8 + a * 2 + p % 2

    mine = channel(pos, y)
    group = (z + x) % 4

    def send_group(step, send_one, self_one):
        def one(q):
            xs = (x + (q // 2) % 4) % 4
            p = ((group + step + 4 - xs) % 4) * 8 + xs * 2 + (c + q % 2) % 2
            send_one(p, (y + q // 8) % 4)

        if step % 4 == 0:
            self_one()
            loop(1, CHUNK, one)
        else:
            loop(0, CHUNK, one)

    def group_rows(zc):
        return [
            pl.ds(pl.multiple_of((((zc + 4 - xs) % 4) * 8 + xs * 2) * ROWS, 2 * ROWS), 2 * ROWS)
            for xs in range(4)
        ]

    loads = [
        pltpu.make_async_copy(src, dst, load_sem.at[n])
        for n, (src, dst) in enumerate(
            (
                (feat_hbm, feat_ref),
                (aw_hbm, aw_ref),
                (tok_hbm, tok_ref),
                (lw_hbm, lw_ref),
                (rw_hbm, rw_ref),
                (iw_hbm, iw_ref),
                (ow_hbm, ow_ref),
                (pair_hbm, pair_ref),
                (cot_hbm, cot_ref),
            )
        )
    ]
    for load in loads:
        load.start()
    barrier = pltpu.get_barrier_semaphore()
    block = me // PAIR_DEV
    place = me % PAIR_DEV
    lead_right = ((place == 0) & (me > 0)).astype(jnp.int32)
    lead_left = ((y == 0) & (pos > 0)).astype(jnp.int32)

    def greet(to):
        @pl.when(to != me)
        def _():
            pl.semaphore_signal(
                barrier,
                inc=1,
                device_id=(to // ATOM_DEV, to % ATOM_DEV),
                device_id_type=pl.DeviceIdType.MESH,
            )

    loop(0, PAIR_DEV, lambda q: greet(y * PAIR_DEV + (place + q) % PAIR_DEV))
    loop(1, ATOM_DEV, lambda q: greet(pos * ATOM_DEV + (y + q) % ATOM_DEV))
    loop(0, ATOM_DEV, lambda q: greet(q * PAIR_DEV + pos))

    @pl.when(y < ATOM_DEV - 1)
    def _():
        greet((y + 1) * PAIR_DEV)

    @pl.when(pos < PAIR_DEV - 1)
    def _():
        greet((pos + 1) * ATOM_DEV)

    greeted = (
        PAIR_DEV
        - (block == y).astype(jnp.int32)
        + ATOM_DEV
        - 1
        + ATOM_DEV
        - (place == pos).astype(jnp.int32)
        + lead_right * (PAIR_DEV - (block == y + 1).astype(jnp.int32))
        + lead_left * ATOM_DEV
    )

    for load in loads[:5]:
        load.wait()

    atom_pre = dot_nn(feat_ref[...], aw_ref[...])
    atom_sig = sigmoid(atom_pre)
    atom_hidden = (atom_pre * atom_sig).astype(BF16)
    dsilu_ref[...] = atom_sig * (1.0 + atom_pre * (1.0 - atom_sig))
    slot = lax.broadcasted_iota(jnp.int32, (1, DEV), 1)
    live_count = jnp.full((1, DEV), 0, jnp.int32)
    for w in range(4):
        live_count = jnp.where(slot // WIN == w, count_ref[w], live_count)
    live = slot % WIN < live_count
    row8 = lax.broadcasted_iota(jnp.int32, (8, DEV), 0)
    lane8 = lax.broadcasted_iota(jnp.int32, (8, DEV), 1)
    member = jnp.where(
        (tok_ref[...] == me * 4 - 1 + row8) & (row8 < 5) & live, F32(1.0), F32(0.0)
    )
    member_ref[...] = member
    high, low = split(dot_nn(member.astype(BF16), atom_hidden))
    counts = jnp.sum(member, axis=1, keepdims=True)
    count_row = jnp.sum(jnp.where(lane8 == row8, counts, 0.0), axis=0, keepdims=True)
    for n, w_ref in enumerate((lw_ref, rw_ref)):
        weight = w_ref[...]
        sums = dot_nn(high, weight) + dot_nn(low, weight)
        bias_msg[n] = jnp.where(row8 == 5, count_row, sums)

    for load in loads[5:]:
        load.wait()
    for q in range(4):
        turned = iw_ref[:, q * CH : (q + 1) * CH].astype(F32).T.astype(BF16)
        for zc in range(4):
            part = turned[zc * CHUNK : (zc + 1) * CHUNK, :]
            at = slice((q % 2) * CHUNK, (q % 2 + 1) * CHUNK)
            wt_ref[q // 2, zc, 0, at, :] = part
            wt_ref[q // 2, (zc + 3) % 4, 1, at, :] = part
    wt5_ref[...] = iw_ref[:, 4 * CH :].astype(F32).T.astype(BF16)
    mt_ref[...] = ow_ref[...].astype(F32).T.astype(BF16)


    pl.semaphore_wait(barrier, greeted)

    right_src = bias_msg.at[1, pl.ds(0, BIAS_ROWS)]
    right_dst = right_in.at[pl.ds(pl.multiple_of(place * 8, 8), BIAS_ROWS)]
    right_self = block == y
    either(right_src, right_dst, 0, pos, block, right_self)
    loop(1, PAIR_DEV, lambda q: remote(right_src, right_dst, 0, (pos + q) % PAIR_DEV, block))
    right_lead = (place == 0) & (me > 0)
    right_lead_self = right_lead & (block - 1 == y)

    @pl.when(right_lead)
    def _():
        lead_dst = right_in.at[pl.ds(PAIR_DEV * 8, BIAS_ROWS)]
        either(right_src, lead_dst, 1, pos, block - 1, block - 1 == y)
        loop(
            1, PAIR_DEV, lambda q: remote(right_src, lead_dst, 1, (pos + q) % PAIR_DEV, block - 1)
        )

    left_src = bias_msg.at[0, pl.ds(0, BIAS_ROWS)]
    left_dst = left_in.at[pl.ds(pl.multiple_of(y * 8, 8), BIAS_ROWS)]
    local(left_src, left_dst, 2)
    loop(1, ATOM_DEV, lambda q: remote(left_src, left_dst, 2, pos, (y + q) % ATOM_DEV))
    left_lead = (y == 0) & (pos > 0)

    @pl.when(left_lead)
    def _():
        loop(
            0,
            ATOM_DEV,
            lambda q: remote(
                left_src,
                left_in.at[pl.ds(ATOM_DEV * 8, BIAS_ROWS)],
                3,
                pos - 1,
                (y + q) % ATOM_DEV,
            ),
        )

    @pl.when(y == ATOM_DEV - 1)
    def _():
        right_in[pl.ds(PAIR_DEV * 8, 8), :] = jnp.zeros((8, CH), F32)

    @pl.when(pos == PAIR_DEV - 1)
    def _():
        left_in[pl.ds(ATOM_DEV * 8, 8), :] = jnp.zeros((8, CH), F32)

    wait_recv(right_in.at[pl.ds(0, PAIR_DEV * BIAS_ROWS)], 0)

    @pl.when(y < ATOM_DEV - 1)
    def _():
        wait_recv(right_in.at[pl.ds(PAIR_DEV * 8, BIAS_ROWS)], 1)

    wait_recv(left_in.at[pl.ds(0, ATOM_DEV * BIAS_ROWS)], 2)

    @pl.when(pos < PAIR_DEV - 1)
    def _():
        wait_recv(left_in.at[pl.ds(ATOM_DEV * 8, BIAS_ROWS)], 3)


    def finish_bias(src, bias_ref, inverse_ref, n):
        lane = lax.broadcasted_iota(jnp.int32, (n, CH), 1)
        count_own = src[pl.ds(5, n, stride=8), :]
        count_next = src[pl.ds(13, n, stride=8), :]
        for q in range(4):
            total = src[pl.ds(1 + q, n, stride=8), :]
            number = jnp.where(lane == 1 + q, count_own, 0.0)
            if q == 3:
                total = total + src[pl.ds(8, n, stride=8), :]
                number = number + jnp.where(lane == 0, count_next, 0.0)
            inverse = 1.0 / jnp.sum(number, axis=1, keepdims=True)
            bias_ref[pl.ds(q, n, stride=4), :] = (total * inverse).astype(BF16).astype(F32)
            inverse_ref[pl.ds(q, n, stride=4), :] = jnp.broadcast_to(inverse, (n, CH))

    finish_bias(right_in, right_bias, right_inv, PAIR_DEV)
    finish_bias(left_in, left_bias, left_inv, ATOM_DEV)


    def front(r):
        values = pair_ref[r].astype(F32) + left_bias[pl.ds(r, 1), :] + right_bias[...]
        values = values.T
        centre = jnp.mean(values, axis=0, keepdims=True)
        shifted = values - centre
        inverse = lax.rsqrt(jnp.mean(shifted * shifted, axis=0, keepdims=True) + EPSILON)
        normed = shifted * inverse
        normed_ref[r] = normed
        inv_ref[pl.ds(r, 1), :] = inverse
        hidden_ref[r] = normed.astype(BF16)

    loop(0, ROWS, front, UNROLL)


    rows_here = pl.ds(pl.multiple_of(pos * ROWS, ROWS), ROWS)
    for side, sig_ref, der_ref, work in (
        (1, sig_right, der_right, work_b),
        (0, sig_left, der_left, work_a),
    ):
        edge_dst = edge_in.at[side, y, rows_here]
        for half in range(2):
            groups = [(group + 2 * half + n) % 4 for n in range(2)]
            firsts = [pl.multiple_of(zc * CHUNK, CHUNK) for zc in groups]

            def edges(r):
                weight = wt_ref[side, groups[0]].reshape(4 * CHUNK, CH)
                pre = dot_nn(weight, hidden_ref[r])
                for n in range(2):
                    value = pre[2 * n * CHUNK : (2 * n + 1) * CHUNK]
                    opened = sigmoid(pre[(2 * n + 1) * CHUNK : (2 * n + 2) * CHUNK])
                    edge = opened * value
                    work[pl.ds(n * CHUNK * ROWS + r, CHUNK, stride=ROWS), :] = edge
                    sig_ref[r, pl.ds(firsts[n], CHUNK), :] = opened
                    der_ref[r, pl.ds(firsts[n], CHUNK), :] = edge * (1.0 - opened)

            loop(0, ROWS, edges, UNROLL)
            for n in range(2):
                edge_out[side, pl.ds(firsts[n], CHUNK)] = (
                    work[n * CHUNK * ROWS : (n + 1) * CHUNK * ROWS, :]
                    .reshape(CHUNK, ROWS, COLS)
                    .astype(BF16)
                )
                step = 2 * half + n
                sem = 4 if side == 1 else 13 + step
                send_group(
                    step,
                    lambda p, a: remote(edge_out.at[side, channel(p, a)], edge_dst, sem, p, a),
                    lambda: local(edge_out.at[side, mine], edge_dst, sem),
                )

    def gate(r):
        opened = sigmoid(dot_nn(wt5_ref[...], hidden_ref[r]))
        gated = cot_ref[r].astype(F32).T * opened
        gate_ref[r] = gated * (1.0 - opened)
        gn_ref[pl.ds(r, CH, stride=ROWS), :] = dot_nn(ow_ref[...], gated.astype(BF16))

    loop(0, ROWS, gate, UNROLL)

    def total(i, acc):
        chunk = gn_ref[pl.ds(pl.multiple_of(i * 128, 128), 128), :].reshape(8, ROWS, COLS)
        return acc + jnp.sum(chunk, axis=0)

    zero = jnp.zeros((ROWS, COLS), F32)
    gn_mean = lax.fori_loop(0, 16, total, zero) * (1.0 / CH)


    prod_dst = prod_in.at[mine]

    def block_of(ref, p, a):
        return ref.at[a, pl.ds(pl.multiple_of(p * ROWS, ROWS), ROWS)]

    wait_recv(edge_in.at[1], 4)
    for step in range(4):
        wait_recv(edge_in.at[0, 0], 13 + step)
        rows = group_rows((group + 4 - step) % 4)
        product = None
        for a in range(4):
            lhs = jnp.concatenate([edge_in[0, a, run, :] for run in rows], axis=0)
            term = dot_nt(lhs, edge_in[1, a])
            product = term if product is None else product + term
        product = product.astype(BF16)
        for a in range(4):
            for n, run in enumerate(rows):
                prod_out[a, run, :] = product[
                    2 * ROWS * n : 2 * ROWS * (n + 1), COLS * a : COLS * (a + 1)
                ]
        send_group(
            (4 - step) % 4,
            lambda p, a: remote(block_of(prod_out, p, a), prod_dst, 5, p, a),
            lambda: local(block_of(prod_out, pos, y), prod_dst, 5),
        )
    wait_recv(prod_in, 5)

    def sum_prod(i, acc):
        return acc + jnp.sum(prod_in[pl.ds(i * 8, 8)].astype(F32), axis=0)

    prod_mean = lax.fori_loop(0, 16, sum_prod, zero) * (1.0 / CH)

    def sum_squares(i, carry):
        squares, cross = carry
        shifted = prod_in[pl.ds(i * 8, 8)].astype(F32) - prod_mean[None]
        upstream = gn_ref[pl.ds(pl.multiple_of(i * 128, 128), 128), :].reshape(8, ROWS, COLS)
        return (
            squares + jnp.sum(shifted * shifted, axis=0),
            cross + jnp.sum(upstream * shifted, axis=0),
        )

    squares, cross = lax.fori_loop(0, 16, sum_squares, (zero, zero))
    prod_inv = lax.rsqrt(squares * (1.0 / CH) + EPSILON)
    cross = cross * prod_inv * prod_inv * (1.0 / CH)


    gp_dst = gp_in.at[y, rows_here]
    for step in range(4):
        zc = (group + step) % 4

        def grads(i):
            at = zc * CHUNK + i * 8
            shifted = prod_in[pl.ds(at, 8)].astype(F32) - prod_mean[None]
            upstream = gn_ref[pl.ds(pl.multiple_of(at * ROWS, 128), 128), :]
            upstream = upstream.reshape(8, ROWS, COLS)
            grad = prod_inv[None] * (upstream - gn_mean[None] - shifted * cross[None])
            gp_out[pl.ds(at, 8)] = grad.astype(BF16)

        loop(0, 4, grads, 4)
        send_group(
            step,
            lambda p, a: remote(gp_out.at[channel(p, a)], gp_dst, 17 + step, p, a),
            lambda: local(gp_out.at[mine], gp_dst, 17 + step),
        )


    left_dst = grad_in.at[0, mine]
    for step in range(4):
        wait_recv(gp_in.at[0], 17 + step)
        rows = group_rows((group + 4 - step) % 4)
        lhs = jnp.concatenate(
            [jnp.concatenate([gp_in[a, run, :] for run in rows], axis=0) for a in range(4)], axis=1
        )
        for a in range(4):
            grad = dot_nn(lhs, edge_in[1, a]).astype(BF16)
            for n, run in enumerate(rows):
                grad_out[0, a, run, :] = grad[2 * ROWS * n : 2 * ROWS * (n + 1), :]
        send_group(
            (4 - step) % 4,
            lambda p, a: remote(block_of(grad_out.at[0], p, a), left_dst, 7, p, a),
            lambda: local(block_of(grad_out.at[0], pos, y), left_dst, 7),
        )
    for zc in range(4):
        lhs = gp_in[zc].T
        for a in range(4):
            grad_out[1, a, 128 * zc : 128 * (zc + 1), :] = dot_nn(lhs, edge_in[0, a]).astype(BF16)
    right_dst = grad_in.at[1, mine]
    for step in range(4):
        send_group(
            step,
            lambda p, a: remote(block_of(grad_out.at[1], p, a), right_dst, 8, p, a),
            lambda: local(block_of(grad_out.at[1], pos, y), right_dst, 8),
        )

    def lay_normed(i):
        shifted = (prod_in[pl.ds(i * 8, 8)].astype(F32) - prod_mean[None]) * prod_inv[None]
        work_a[pl.ds(pl.multiple_of(i * 128, 128), 128), :] = shifted.reshape(128, COLS)

    loop(0, 16, lay_normed, UNROLL)

    def gate_grad(r):
        normed = work_a[pl.ds(r, CH, stride=ROWS), :].astype(BF16)
        gg_ref[r] = (dot_nn(mt_ref[...], normed) * gate_ref[r]).astype(BF16)

    loop(0, ROWS, gate_grad, UNROLL)


    row_ext[...] = jnp.zeros_like(row_ext)
    col_ext[...] = jnp.zeros_like(col_ext)
    col_acc[...] = jnp.zeros_like(col_acc)

    def lay_grads(side, work):
        def lay(i):
            work[pl.ds(pl.multiple_of(i * 128, 128), 128), :] = (
                grad_in[side, pl.ds(i * 8, 8)].astype(F32).reshape(128, COLS)
            )

        loop(0, 16, lay, UNROLL)

    def branches(work, sig_ref, der_ref, r):
        flow = work[pl.ds(r, CH, stride=ROWS), :]
        return [(flow * sig_ref[r]).astype(BF16), (flow * der_ref[r]).astype(BF16)]

    def partial(r):
        left = branches(work_a, sig_left, der_left, r)
        gate_ref[r] = dot_nn(iw_ref[:, : 2 * CH], jnp.concatenate(left, axis=0)) + dot_nn(
            iw_ref[:, 4 * CH :], gg_ref[r]
        )

    wait_recv(grad_in.at[0], 7)
    lay_grads(0, work_a)
    loop(0, ROWS, partial, UNROLL)
    wait_recv(grad_in.at[1], 8)
    lay_grads(1, work_b)

    def last(r):
        right = branches(work_b, sig_right, der_right, r)
        grad = gate_ref[r] + dot_nn(iw_ref[:, 2 * CH : 4 * CH], jnp.concatenate(right, axis=0))
        normed = normed_ref[r]
        first_mean = jnp.mean(grad, axis=0, keepdims=True)
        cross_mean = jnp.mean(grad * normed, axis=0, keepdims=True)
        grad = inv_ref[pl.ds(r, 1), :] * (grad - first_mean - normed * cross_mean)
        grad = grad.T
        pg_ref[r] = grad.astype(BF16)
        col_acc[...] += grad
        row_ext[pl.ds(8 + r, 1), :] = jnp.sum(grad, axis=0, keepdims=True)

    loop(0, ROWS, last, UNROLL)


    store = pltpu.make_async_copy(pg_ref, pg_hbm, load_sem.at[9])
    store.start()

    row_ext[8:24, :] = row_ext[8:24, :] * left_inv[...]
    col_ext[8:136, :] = col_acc[...] * right_inv[...]
    for m in range(ATOM_DEV + 1):
        row_msg[m] = row_ext[7 + 4 * m : 15 + 4 * m, :]
    for m in range(PAIR_DEV + 1):
        col_msg[m] = col_ext[7 + 4 * m : 15 + 4 * m, :]

    used = pl.ds(0, SUM_ROWS)
    local(row_msg.at[y, used], row_in.at[y, used], 9)

    def send_row(q):
        a = (y + q) % ATOM_DEV
        remote(row_msg.at[a, used], row_in.at[y, used], 9, pos, a)

    loop(1, ATOM_DEV, send_row)
    row_lead = pos < PAIR_DEV - 1

    @pl.when(row_lead)
    def _():
        remote(row_msg.at[ATOM_DEV, used], row_in.at[ATOM_DEV + y, used], 10, pos + 1, 0)

    def send_col(q):
        m = (place + q) % PAIR_DEV
        p = y * 8 + m // 4
        a = m % 4
        either(col_msg.at[m, used], col_in.at[pos, used], 11, p, a, (p == pos) & (a == y))

    loop(0, PAIR_DEV, send_col)
    col_lead = y < ATOM_DEV - 1
    col_lead_self = col_lead & (pos == (y + 1) * 8) & (y == 0)

    @pl.when(col_lead)
    def _():
        either(
            col_msg.at[PAIR_DEV, used],
            col_in.at[PAIR_DEV + pos, used],
            12,
            (y + 1) * 8,
            0,
            col_lead_self,
        )

    row_more = (y == 0) & (pos > 0)
    col_more = (place == 0) & (me > 0)

    @pl.when(jnp.logical_not(row_more))
    def _():
        row_in[ATOM_DEV:] = jnp.zeros((ATOM_DEV, 8, CH), F32)

    @pl.when(jnp.logical_not(col_more))
    def _():
        col_in[PAIR_DEV:] = jnp.zeros((PAIR_DEV, 8, CH), F32)

    wait_recv(row_in.at[pl.ds(0, ATOM_DEV), used], 9)

    @pl.when(row_more)
    def _():
        wait_recv(row_in.at[pl.ds(ATOM_DEV, ATOM_DEV), used], 10)

    wait_recv(col_in.at[pl.ds(0, PAIR_DEV), used], 11)

    @pl.when(col_more)
    def _():
        wait_recv(col_in.at[pl.ds(PAIR_DEV, PAIR_DEV), used], 12)


    single = jnp.zeros((8, 3 * CH), F32)
    for ref, w_ref in ((row_in, lw_ref), (col_in, rw_ref)):
        weight = w_ref[...]
        sums = jnp.where(row8 < SUM_ROWS, jnp.sum(ref[...], axis=0), 0.0)
        for part in split(sums):
            single = single + dot_nt(part, weight)
    picked = dot_tn(member_ref[...].astype(BF16), single.astype(BF16))
    atom_grad = (picked * dsilu_ref[...]).astype(BF16)
    ag_ref[...] = dot_nt(atom_grad, aw_ref[...]).astype(BF16)

    store.wait()

    wait_send(right_in.at[pl.ds(0, (PAIR_DEV - 1) * BIAS_ROWS)], 0)

    @pl.when(jnp.logical_not(right_self))
    def _():
        wait_send(right_in.at[pl.ds(0, BIAS_ROWS)], 0)

    @pl.when(right_lead)
    def _():
        wait_send(right_in.at[pl.ds(0, (PAIR_DEV - 1) * BIAS_ROWS)], 1)

        @pl.when(jnp.logical_not(right_lead_self))
        def _():
            wait_send(right_in.at[pl.ds(0, BIAS_ROWS)], 1)

    wait_send(left_in.at[pl.ds(0, (ATOM_DEV - 1) * BIAS_ROWS)], 2)

    @pl.when(left_lead)
    def _():
        wait_send(left_in.at[pl.ds(0, ATOM_DEV * BIAS_ROWS)], 3)

    wait_send(edge_out.at[1, pl.ds(0, DEV - 1)], 4)
    for step in range(4):
        sent = pl.ds(0, CHUNK - 1 if step == 0 else CHUNK)
        wait_send(edge_out.at[0, sent], 13 + step)
        wait_send(gp_out.at[sent], 17 + step)
    wait_send(prod_in.at[pl.ds(0, DEV - 1)], 5)
    for side in range(2):
        wait_send(grad_in.at[side, pl.ds(0, DEV - 1)], 7 + side)
    wait_send(row_msg.at[pl.ds(0, ATOM_DEV - 1), used], 9)

    @pl.when(row_lead)
    def _():
        wait_send(row_msg.at[pl.ds(0, 1), used], 10)

    wait_send(col_msg.at[pl.ds(0, PAIR_DEV - 1), used], 11)

    @pl.when(block != y)
    def _():
        wait_send(col_msg.at[pl.ds(0, 1), used], 11)

    @pl.when(col_lead & jnp.logical_not(col_lead_self))
    def _():
        wait_send(col_msg.at[pl.ds(0, 1), used], 12)


def body(
    pair_state,
    cotangent,
    atom_feats,
    atom_token,
    window_count,
    input_weight,
    output_weight,
    atom_weight,
    left_weight,
    right_weight,
):
    vmem = pl.BlockSpec(memory_space=pltpu.VMEM)
    hbm = pl.BlockSpec(memory_space=pl.ANY)
    rows = (ROWS, CH, COLS)
    scratch = [
        (rows, BF16),
        (rows, BF16),
        ((DEV, CH), BF16),
        ((1, DEV), jnp.int32),
        ((CH, 5 * CH), BF16),
        ((CH, CH), BF16),
        ((CH, 3 * CH), BF16),
        ((3 * CH, CH), BF16),
        ((3 * CH, CH), BF16),
        ((8, DEV), F32),
        ((DEV, 3 * CH), F32),
        ((2, 8, CH), F32),
        (((PAIR_DEV + 1) * 8 + 8, CH), F32),
        (((ATOM_DEV + 1) * 8 + 8, CH), F32),
        ((COLS, CH), F32),
        ((COLS, CH), F32),
        ((ROWS, CH), F32),
        ((ROWS, CH), F32),
        ((2, 4, 2, 2 * CHUNK, CH), BF16),
        ((CH, CH), BF16),
        ((CH, CH), BF16),
        (rows, F32),
        ((ROWS, COLS), F32),
        (rows, BF16),
        (rows, F32),
        (rows, F32),
        (rows, F32),
        (rows, F32),
        (rows, F32),
        ((CH * ROWS, COLS), F32),
        (rows, BF16),
        ((CH * ROWS, COLS), F32),
        ((CH * ROWS, COLS), F32),
        ((2, DEV, ROWS, COLS), BF16),
        ((2, 4, TOK, COLS), BF16),
        ((4, TOK, COLS), BF16),
        ((DEV, ROWS, COLS), BF16),
        ((DEV, ROWS, COLS), BF16),
        ((4, TOK, COLS), BF16),
        ((2, 4, TOK, COLS), BF16),
        ((2, DEV, ROWS, COLS), BF16),
        (rows, BF16),
        ((COLS, CH), F32),
        ((40, CH), F32),
        ((152, CH), F32),
        ((ATOM_DEV + 1, 8, CH), F32),
        ((PAIR_DEV + 1, 8, CH), F32),
        ((2 * ATOM_DEV, 8, CH), F32),
        ((2 * PAIR_DEV, 8, CH), F32),
    ]
    return pl.pallas_call(
        kernel,
        out_shape=(
            jax.ShapeDtypeStruct(pair_state.shape, BF16),
            jax.ShapeDtypeStruct(atom_feats.shape, BF16),
        ),
        in_specs=[hbm] * 4 + [pl.BlockSpec(memory_space=pltpu.SMEM)] + [hbm] * 5,
        out_specs=(hbm, vmem),
        scratch_shapes=[pltpu.VMEM(shape, dtype) for shape, dtype in scratch]
        + [pltpu.SemaphoreType.DMA((n,)) for n in (21, 21, 10)],
        compiler_params=pltpu.CompilerParams(
            collective_id=0, has_side_effects=True, vmem_limit_bytes=60 * 2**20
        ),
        cost_estimate=pl.CostEstimate(
            flops=1_700_000_000, bytes_accessed=2**21, transcendentals=2**20
        ),
    )(
        pair_state,
        cotangent,
        atom_feats,
        atom_token.reshape(1, -1),
        window_count,
        input_weight,
        output_weight,
        atom_weight,
        left_weight,
        right_weight,
    )


def solution(mesh):
    placed = (
        P("pair", "atom", None),
        P("pair", "atom", None),
        P(("pair", "atom"), None),
        P(("pair", "atom")),
        P(("pair", "atom")),
        P(),
        P(),
        P(),
        P(),
        P(),
    )
    return jax.shard_map(
        body,
        mesh=mesh,
        in_specs=placed,
        out_specs=(P("pair", "atom", None), P(("pair", "atom"), None)),
        check_vma=False,
    )
```

```python
import jax
import jax.numpy as jnp
from jax import lax
from jax.experimental import pallas as pl
from jax.experimental.pallas import tpu as pltpu
from jax.sharding import PartitionSpec as P

EPSILON = 1e-05
F32 = jnp.float32
BF16 = jnp.bfloat16
ROWS = 16
COLS = 128
CH = 128
DEV = 128
TOK = 512
WIN = 32
PAIR_DEV = 32
ATOM_DEV = 4
CHUNK = 32
UNROLL = 16
BIAS_ROWS = 6
SUM_ROWS = 5
PARTS = 4


def dot_nn(a, b):
    return lax.dot_general(a, b, (((1,), (0,)), ((), ())), preferred_element_type=F32)


def dot_nt(a, b):
    return lax.dot_general(a, b, (((1,), (1,)), ((), ())), preferred_element_type=F32)


def dot_tn(a, b):
    return lax.dot_general(a, b, (((0,), (0,)), ((), ())), preferred_element_type=F32)


def split(x):
    high = x.astype(BF16)
    return high, (x - high.astype(F32)).astype(BF16)


def sigmoid(x):
    return 0.5 * jnp.tanh(0.5 * x) + 0.5


def loop(start, stop, step, unroll=1):
    def run(i, carry):
        step(i)
        return carry

    lax.fori_loop(start, stop, run, 0, unroll=unroll)


def kernel(
    pair_hbm,
    cot_hbm,
    feat_hbm,
    tok_hbm,
    count_ref,
    iw_hbm,
    ow_hbm,
    aw_hbm,
    lw_hbm,
    rw_hbm,
    pg_hbm,
    ag_ref,
    pair_ref,
    cot_ref,
    feat_ref,
    tok_ref,
    iw_ref,
    ow_ref,
    aw_ref,
    lw_ref,
    rw_ref,
    member_ref,
    dsilu_ref,
    bias_msg,
    right_in,
    left_in,
    right_bias,
    right_inv,
    left_bias,
    left_inv,
    wt_ref,
    wt5_ref,
    mt_ref,
    normed_ref,
    inv_ref,
    hidden_ref,
    sig_left,
    sig_right,
    der_left,
    der_right,
    gate_ref,
    gn_ref,
    gg_ref,
    work_a,
    work_b,
    edge_out,
    edge_in,
    prod_out,
    prod_in,
    gp_out,
    gp_in,
    grad_out,
    grad_in,
    pg_ref,
    col_acc,
    row_ext,
    col_ext,
    row_msg,
    col_msg,
    row_in,
    col_in,
    send_sem,
    recv_sem,
    load_sem,
):
    pos = lax.axis_index("pair")
    y = lax.axis_index("atom")
    me = pos * ATOM_DEV + y
    z = pos // 8
    x = (pos // 2) % 4
    c = pos % 2

    def remote(src, dst, sem, p, a):
        pltpu.make_async_remote_copy(
            src_ref=src,
            dst_ref=dst,
            send_sem=send_sem.at[sem],
            recv_sem=recv_sem.at[sem],
            device_id=(p, a),
            device_id_type=pl.DeviceIdType.MESH,
        ).start()

    def local(src, dst, sem):
        pltpu.make_async_copy(src, dst, recv_sem.at[sem]).start()

    def either(src, dst, sem, p, a, is_self):
        @pl.when(is_self)
        def _():
            local(src, dst, sem)

        @pl.when(jnp.logical_not(is_self))
        def _():
            remote(src, dst, sem, p, a)

    def wait_recv(ref, sem):
        pltpu.make_async_copy(ref, ref, recv_sem.at[sem]).wait()

    def wait_send(ref, sem):
        pltpu.make_async_copy(ref, ref, send_sem.at[sem]).wait()

    def channel(p, a):
        return ((p // 8 + (p // 2) % 4) % 4) * CHUNK + ((p // 2) % 4) * 8 + a * 2 + p % 2

    mine = channel(pos, y)
    group = (z + x) % 4

    def send_group(step, send_one, self_one):
        def one(q):
            xs = (x + (q // 2) % 4) % 4
            p = ((group + step + 4 - xs) % 4) * 8 + xs * 2 + (c + q % 2) % 2
            send_one(p, (y + q // 8) % 4)

        if step % 4 == 0:
            self_one()
            loop(1, CHUNK, one)
        else:
            loop(0, CHUNK, one)

    def group_rows(zc):
        return [
            pl.ds(pl.multiple_of((((zc + 4 - xs) % 4) * 8 + xs * 2) * ROWS, 2 * ROWS), 2 * ROWS)
            for xs in range(4)
        ]

    loads = [
        pltpu.make_async_copy(src, dst, load_sem.at[n])
        for n, (src, dst) in enumerate(
            (
                (feat_hbm, feat_ref),
                (aw_hbm, aw_ref),
                (tok_hbm, tok_ref),
                (lw_hbm, lw_ref),
                (rw_hbm, rw_ref),
                (iw_hbm, iw_ref),
                (ow_hbm, ow_ref),
                (pair_hbm, pair_ref),
                (cot_hbm, cot_ref),
            )
        )
    ]
    for load in loads:
        load.start()
    barrier = pltpu.get_barrier_semaphore()
    block = me // PAIR_DEV
    place = me % PAIR_DEV
    lead_right = ((place == 0) & (me > 0)).astype(jnp.int32)
    lead_left = ((y == 0) & (pos > 0)).astype(jnp.int32)

    def greet(to):
        @pl.when(to != me)
        def _():
            pl.semaphore_signal(
                barrier,
                inc=1,
                device_id=(to // ATOM_DEV, to % ATOM_DEV),
                device_id_type=pl.DeviceIdType.MESH,
            )

    loop(0, PAIR_DEV, lambda q: greet(y * PAIR_DEV + (place + q) % PAIR_DEV))
    loop(1, ATOM_DEV, lambda q: greet(pos * ATOM_DEV + (y + q) % ATOM_DEV))
    loop(0, ATOM_DEV, lambda q: greet(q * PAIR_DEV + pos))

    @pl.when(y < ATOM_DEV - 1)
    def _():
        greet((y + 1) * PAIR_DEV)

    @pl.when(pos < PAIR_DEV - 1)
    def _():
        greet((pos + 1) * ATOM_DEV)

    greeted = (
        PAIR_DEV
        - (block == y).astype(jnp.int32)
        + ATOM_DEV
        - 1
        + ATOM_DEV
        - (place == pos).astype(jnp.int32)
        + lead_right * (PAIR_DEV - (block == y + 1).astype(jnp.int32))
        + lead_left * ATOM_DEV
    )

    for load in loads[:5]:
        load.wait()

    atom_pre = dot_nn(feat_ref[...], aw_ref[...])
    atom_sig = sigmoid(atom_pre)
    atom_hidden = (atom_pre * atom_sig).astype(BF16)
    dsilu_ref[...] = atom_sig * (1.0 + atom_pre * (1.0 - atom_sig))
    slot = lax.broadcasted_iota(jnp.int32, (1, DEV), 1)
    live_count = jnp.full((1, DEV), 0, jnp.int32)
    for w in range(4):
        live_count = jnp.where(slot // WIN == w, count_ref[w], live_count)
    live = slot % WIN < live_count
    row8 = lax.broadcasted_iota(jnp.int32, (8, DEV), 0)
    lane8 = lax.broadcasted_iota(jnp.int32, (8, DEV), 1)
    member = jnp.where(
        (tok_ref[...] == me * 4 - 1 + row8) & (row8 < 5) & live, F32(1.0), F32(0.0)
    )
    member_ref[...] = member
    high, low = split(dot_nn(member.astype(BF16), atom_hidden))
    counts = jnp.sum(member, axis=1, keepdims=True)
    count_row = jnp.sum(jnp.where(lane8 == row8, counts, 0.0), axis=0, keepdims=True)
    for n, w_ref in enumerate((lw_ref, rw_ref)):
        weight = w_ref[...]
        sums = dot_nn(high, weight) + dot_nn(low, weight)
        bias_msg[n] = jnp.where(row8 == 5, count_row, sums)

    for load in loads[5:]:
        load.wait()
    for q in range(4):
        turned = iw_ref[:, q * CH : (q + 1) * CH].astype(F32).T.astype(BF16)
        for zc in range(4):
            part = turned[zc * CHUNK : (zc + 1) * CHUNK, :]
            at = slice((q % 2) * CHUNK, (q % 2 + 1) * CHUNK)
            wt_ref[q // 2, zc, 0, at, :] = part
            wt_ref[q // 2, (zc + 3) % 4, 1, at, :] = part
    wt5_ref[...] = iw_ref[:, 4 * CH :].astype(F32).T.astype(BF16)
    mt_ref[...] = ow_ref[...].astype(F32).T.astype(BF16)


    pl.semaphore_wait(barrier, greeted)

    right_src = bias_msg.at[1, pl.ds(0, BIAS_ROWS)]
    right_dst = right_in.at[pl.ds(pl.multiple_of(place * 8, 8), BIAS_ROWS)]
    right_self = block == y
    either(right_src, right_dst, 0, pos, block, right_self)
    loop(1, PAIR_DEV, lambda q: remote(right_src, right_dst, 0, (pos + q) % PAIR_DEV, block))
    right_lead = (place == 0) & (me > 0)
    right_lead_self = right_lead & (block - 1 == y)

    @pl.when(right_lead)
    def _():
        lead_dst = right_in.at[pl.ds(PAIR_DEV * 8, BIAS_ROWS)]
        either(right_src, lead_dst, 1, pos, block - 1, block - 1 == y)
        loop(
            1, PAIR_DEV, lambda q: remote(right_src, lead_dst, 1, (pos + q) % PAIR_DEV, block - 1)
        )

    left_src = bias_msg.at[0, pl.ds(0, BIAS_ROWS)]
    left_dst = left_in.at[pl.ds(pl.multiple_of(y * 8, 8), BIAS_ROWS)]
    local(left_src, left_dst, 2)
    loop(1, ATOM_DEV, lambda q: remote(left_src, left_dst, 2, pos, (y + q) % ATOM_DEV))
    left_lead = (y == 0) & (pos > 0)

    @pl.when(left_lead)
    def _():
        loop(
            0,
            ATOM_DEV,
            lambda q: remote(
                left_src,
                left_in.at[pl.ds(ATOM_DEV * 8, BIAS_ROWS)],
                3,
                pos - 1,
                (y + q) % ATOM_DEV,
            ),
        )

    @pl.when(y == ATOM_DEV - 1)
    def _():
        right_in[pl.ds(PAIR_DEV * 8, 8), :] = jnp.zeros((8, CH), F32)

    @pl.when(pos == PAIR_DEV - 1)
    def _():
        left_in[pl.ds(ATOM_DEV * 8, 8), :] = jnp.zeros((8, CH), F32)

    wait_recv(right_in.at[pl.ds(0, PAIR_DEV * BIAS_ROWS)], 0)

    @pl.when(y < ATOM_DEV - 1)
    def _():
        wait_recv(right_in.at[pl.ds(PAIR_DEV * 8, BIAS_ROWS)], 1)

    wait_recv(left_in.at[pl.ds(0, ATOM_DEV * BIAS_ROWS)], 2)

    @pl.when(pos < PAIR_DEV - 1)
    def _():
        wait_recv(left_in.at[pl.ds(ATOM_DEV * 8, BIAS_ROWS)], 3)


    def finish_bias(src, bias_ref, inverse_ref, n):
        lane = lax.broadcasted_iota(jnp.int32, (n, CH), 1)
        count_own = src[pl.ds(5, n, stride=8), :]
        count_next = src[pl.ds(13, n, stride=8), :]
        for q in range(4):
            total = src[pl.ds(1 + q, n, stride=8), :]
            number = jnp.where(lane == 1 + q, count_own, 0.0)
            if q == 3:
                total = total + src[pl.ds(8, n, stride=8), :]
                number = number + jnp.where(lane == 0, count_next, 0.0)
            inverse = 1.0 / jnp.sum(number, axis=1, keepdims=True)
            bias_ref[pl.ds(q, n, stride=4), :] = (total * inverse).astype(BF16).astype(F32)
            inverse_ref[pl.ds(q, n, stride=4), :] = jnp.broadcast_to(inverse, (n, CH))

    finish_bias(right_in, right_bias, right_inv, PAIR_DEV)
    finish_bias(left_in, left_bias, left_inv, ATOM_DEV)


    def front(r):
        values = pair_ref[r].astype(F32) + left_bias[pl.ds(r, 1), :] + right_bias[...]
        values = values.T
        centre = jnp.mean(values, axis=0, keepdims=True)
        shifted = values - centre
        inverse = lax.rsqrt(jnp.mean(shifted * shifted, axis=0, keepdims=True) + EPSILON)
        normed = shifted * inverse
        normed_ref[r] = normed
        inv_ref[pl.ds(r, 1), :] = inverse
        hidden_ref[r] = normed.astype(BF16)

    loop(0, ROWS, front, UNROLL)


    rows_here = pl.ds(pl.multiple_of(pos * ROWS, ROWS), ROWS)
    for side, sig_ref, der_ref, work in (
        (1, sig_right, der_right, work_b),
        (0, sig_left, der_left, work_a),
    ):
        edge_dst = edge_in.at[side, y, rows_here]
        for half in range(2):
            groups = [(group + 2 * half + n) % 4 for n in range(2)]
            firsts = [pl.multiple_of(zc * CHUNK, CHUNK) for zc in groups]

            def edges(r):
                weight = wt_ref[side, groups[0]].reshape(4 * CHUNK, CH)
                pre = dot_nn(weight, hidden_ref[r])
                for n in range(2):
                    value = pre[2 * n * CHUNK : (2 * n + 1) * CHUNK]
                    opened = sigmoid(pre[(2 * n + 1) * CHUNK : (2 * n + 2) * CHUNK])
                    edge = opened * value
                    work[pl.ds(n * CHUNK * ROWS + r, CHUNK, stride=ROWS), :] = edge
                    sig_ref[r, pl.ds(firsts[n], CHUNK), :] = opened
                    der_ref[r, pl.ds(firsts[n], CHUNK), :] = edge * (1.0 - opened)

            loop(0, ROWS, edges, UNROLL)
            for n in range(2):
                edge_out[side, pl.ds(firsts[n], CHUNK)] = (
                    work[n * CHUNK * ROWS : (n + 1) * CHUNK * ROWS, :]
                    .reshape(CHUNK, ROWS, COLS)
                    .astype(BF16)
                )
                step = 2 * half + n
                sem = 4 if side == 1 else 13 + step
                send_group(
                    step,
                    lambda p, a: remote(edge_out.at[side, channel(p, a)], edge_dst, sem, p, a),
                    lambda: local(edge_out.at[side, mine], edge_dst, sem),
                )

    def gate(r):
        opened = sigmoid(dot_nn(wt5_ref[...], hidden_ref[r]))
        gated = cot_ref[r].astype(F32).T * opened
        gate_ref[r] = gated * (1.0 - opened)
        gn_ref[pl.ds(r, CH, stride=ROWS), :] = dot_nn(ow_ref[...], gated.astype(BF16))

    loop(0, ROWS, gate, UNROLL)

    def total(i, acc):
        chunk = gn_ref[pl.ds(pl.multiple_of(i * 128, 128), 128), :].reshape(8, ROWS, COLS)
        return acc + jnp.sum(chunk, axis=0)

    zero = jnp.zeros((ROWS, COLS), F32)
    gn_mean = lax.fori_loop(0, 16, total, zero) * (1.0 / CH)


    prod_dst = prod_in.at[mine]

    def block_of(ref, p, a):
        return ref.at[a, pl.ds(pl.multiple_of(p * ROWS, ROWS), ROWS)]

    wait_recv(edge_in.at[1], 4)
    for step in range(4):
        wait_recv(edge_in.at[0, 0], 13 + step)
        rows = group_rows((group + 4 - step) % 4)
        product = None
        for a in range(4):
            lhs = jnp.concatenate([edge_in[0, a, run, :] for run in rows], axis=0)
            term = dot_nt(lhs, edge_in[1, a])
            product = term if product is None else product + term
        product = product.astype(BF16)
        for a in range(4):
            for n, run in enumerate(rows):
                prod_out[a, run, :] = product[
                    2 * ROWS * n : 2 * ROWS * (n + 1), COLS * a : COLS * (a + 1)
                ]
        send_group(
            (4 - step) % 4,
            lambda p, a: remote(block_of(prod_out, p, a), prod_dst, 5, p, a),
            lambda: local(block_of(prod_out, pos, y), prod_dst, 5),
        )
    wait_recv(prod_in, 5)

    def sum_prod(i, acc):
        return acc + jnp.sum(prod_in[pl.ds(i * 8, 8)].astype(F32), axis=0)

    prod_mean = lax.fori_loop(0, 16, sum_prod, zero) * (1.0 / CH)

    def sum_squares(i, carry):
        squares, cross = carry
        shifted = prod_in[pl.ds(i * 8, 8)].astype(F32) - prod_mean[None]
        upstream = gn_ref[pl.ds(pl.multiple_of(i * 128, 128), 128), :].reshape(8, ROWS, COLS)
        return (
            squares + jnp.sum(shifted * shifted, axis=0),
            cross + jnp.sum(upstream * shifted, axis=0),
        )

    squares, cross = lax.fori_loop(0, 16, sum_squares, (zero, zero))
    prod_inv = lax.rsqrt(squares * (1.0 / CH) + EPSILON)
    cross = cross * prod_inv * prod_inv * (1.0 / CH)


    gp_dst = gp_in.at[y, rows_here]
    for step in range(4):
        zc = (group + step) % 4

        def grads(i):
            at = zc * CHUNK + i * 8
            shifted = prod_in[pl.ds(at, 8)].astype(F32) - prod_mean[None]
            upstream = gn_ref[pl.ds(pl.multiple_of(at * ROWS, 128), 128), :]
            upstream = upstream.reshape(8, ROWS, COLS)
            grad = prod_inv[None] * (upstream - gn_mean[None] - shifted * cross[None])
            gp_out[pl.ds(at, 8)] = grad.astype(BF16)

        loop(0, 4, grads, 4)
        send_group(
            step,
            lambda p, a: remote(gp_out.at[channel(p, a)], gp_dst, 17 + step, p, a),
            lambda: local(gp_out.at[mine], gp_dst, 17 + step),
        )


    left_dst = grad_in.at[0, mine]
    for step in range(4):
        wait_recv(gp_in.at[0], 17 + step)
        rows = group_rows((group + 4 - step) % 4)
        lhs = jnp.concatenate(
            [jnp.concatenate([gp_in[a, run, :] for run in rows], axis=0) for a in range(4)], axis=1
        )
        for a in range(4):
            grad = dot_nn(lhs, edge_in[1, a]).astype(BF16)
            for n, run in enumerate(rows):
                grad_out[0, a, run, :] = grad[2 * ROWS * n : 2 * ROWS * (n + 1), :]
        send_group(
            (4 - step) % 4,
            lambda p, a: remote(block_of(grad_out.at[0], p, a), left_dst, 7, p, a),
            lambda: local(block_of(grad_out.at[0], pos, y), left_dst, 7),
        )
    for zc in range(4):
        lhs = gp_in[zc].T
        for a in range(4):
            grad_out[1, a, 128 * zc : 128 * (zc + 1), :] = dot_nn(lhs, edge_in[0, a]).astype(BF16)
    right_dst = grad_in.at[1, mine]
    for step in range(4):
        send_group(
            step,
            lambda p, a: remote(block_of(grad_out.at[1], p, a), right_dst, 8, p, a),
            lambda: local(block_of(grad_out.at[1], pos, y), right_dst, 8),
        )

    def lay_normed(i):
        shifted = (prod_in[pl.ds(i * 8, 8)].astype(F32) - prod_mean[None]) * prod_inv[None]
        work_a[pl.ds(pl.multiple_of(i * 128, 128), 128), :] = shifted.reshape(128, COLS)

    loop(0, 16, lay_normed, UNROLL)

    def gate_grad(r):
        normed = work_a[pl.ds(r, CH, stride=ROWS), :].astype(BF16)
        gg_ref[r] = (dot_nn(mt_ref[...], normed) * gate_ref[r]).astype(BF16)

    loop(0, ROWS, gate_grad, UNROLL)


    row_ext[...] = jnp.zeros_like(row_ext)
    col_ext[...] = jnp.zeros_like(col_ext)
    col_acc[...] = jnp.zeros_like(col_acc)

    def lay_grads(side, work):
        def lay(i):
            work[pl.ds(pl.multiple_of(i * 128, 128), 128), :] = (
                grad_in[side, pl.ds(i * 8, 8)].astype(F32).reshape(128, COLS)
            )

        loop(0, 16, lay, UNROLL)

    def branches(work, sig_ref, der_ref, r):
        flow = work[pl.ds(r, CH, stride=ROWS), :]
        return [(flow * sig_ref[r]).astype(BF16), (flow * der_ref[r]).astype(BF16)]

    def partial(r):
        left = branches(work_a, sig_left, der_left, r)
        gate_ref[r] = dot_nn(iw_ref[:, : 2 * CH], jnp.concatenate(left, axis=0)) + dot_nn(
            iw_ref[:, 4 * CH :], gg_ref[r]
        )

    wait_recv(grad_in.at[0], 7)
    lay_grads(0, work_a)
    loop(0, ROWS, partial, UNROLL)
    wait_recv(grad_in.at[1], 8)
    lay_grads(1, work_b)

    def last(r):
        right = branches(work_b, sig_right, der_right, r)
        grad = gate_ref[r] + dot_nn(iw_ref[:, 2 * CH : 4 * CH], jnp.concatenate(right, axis=0))
        normed = normed_ref[r]
        first_mean = jnp.mean(grad, axis=0, keepdims=True)
        cross_mean = jnp.mean(grad * normed, axis=0, keepdims=True)
        grad = inv_ref[pl.ds(r, 1), :] * (grad - first_mean - normed * cross_mean)
        grad = grad.T
        pg_ref[r] = grad.astype(BF16)
        col_acc[...] += grad
        row_ext[pl.ds(8 + r, 1), :] = jnp.sum(grad, axis=0, keepdims=True)

    loop(0, ROWS, last, UNROLL)


    store = pltpu.make_async_copy(pg_ref, pg_hbm, load_sem.at[9])
    store.start()

    row_ext[8:24, :] = row_ext[8:24, :] * left_inv[...]
    col_ext[8:136, :] = col_acc[...] * right_inv[...]
    for m in range(ATOM_DEV + 1):
        row_msg[m] = row_ext[7 + 4 * m : 15 + 4 * m, :]
    for m in range(PAIR_DEV + 1):
        col_msg[m] = col_ext[7 + 4 * m : 15 + 4 * m, :]

    used = pl.ds(0, SUM_ROWS)
    local(row_msg.at[y, used], row_in.at[y, used], 9)

    def send_row(q):
        a = (y + q) % ATOM_DEV
        remote(row_msg.at[a, used], row_in.at[y, used], 9, pos, a)

    loop(1, ATOM_DEV, send_row)
    row_lead = pos < PAIR_DEV - 1

    @pl.when(row_lead)
    def _():
        remote(row_msg.at[ATOM_DEV, used], row_in.at[ATOM_DEV + y, used], 10, pos + 1, 0)

    def send_col(q):
        m = (place + q) % PAIR_DEV
        p = y * 8 + m // 4
        a = m % 4
        either(col_msg.at[m, used], col_in.at[pos, used], 11, p, a, (p == pos) & (a == y))

    loop(0, PAIR_DEV, send_col)
    col_lead = y < ATOM_DEV - 1
    col_lead_self = col_lead & (pos == (y + 1) * 8) & (y == 0)

    @pl.when(col_lead)
    def _():
        either(
            col_msg.at[PAIR_DEV, used],
            col_in.at[PAIR_DEV + pos, used],
            12,
            (y + 1) * 8,
            0,
            col_lead_self,
        )

    row_more = (y == 0) & (pos > 0)
    col_more = (place == 0) & (me > 0)

    @pl.when(jnp.logical_not(row_more))
    def _():
        row_in[ATOM_DEV:] = jnp.zeros((ATOM_DEV, 8, CH), F32)

    @pl.when(jnp.logical_not(col_more))
    def _():
        col_in[PAIR_DEV:] = jnp.zeros((PAIR_DEV, 8, CH), F32)

    wait_recv(row_in.at[pl.ds(0, ATOM_DEV), used], 9)

    @pl.when(row_more)
    def _():
        wait_recv(row_in.at[pl.ds(ATOM_DEV, ATOM_DEV), used], 10)

    wait_recv(col_in.at[pl.ds(0, PAIR_DEV), used], 11)

    @pl.when(col_more)
    def _():
        wait_recv(col_in.at[pl.ds(PAIR_DEV, PAIR_DEV), used], 12)


    single = jnp.zeros((8, 3 * CH), F32)
    for ref, w_ref in ((row_in, lw_ref), (col_in, rw_ref)):
        weight = w_ref[...]
        sums = jnp.where(row8 < SUM_ROWS, jnp.sum(ref[...], axis=0), 0.0)
        for part in split(sums):
            single = single + dot_nt(part, weight)
    picked = dot_tn(member_ref[...].astype(BF16), single.astype(BF16))
    atom_grad = (picked * dsilu_ref[...]).astype(BF16)
    ag_ref[...] = dot_nt(atom_grad, aw_ref[...]).astype(BF16)

    store.wait()

    wait_send(right_in.at[pl.ds(0, (PAIR_DEV - 1) * BIAS_ROWS)], 0)

    @pl.when(jnp.logical_not(right_self))
    def _():
        wait_send(right_in.at[pl.ds(0, BIAS_ROWS)], 0)

    @pl.when(right_lead)
    def _():
        wait_send(right_in.at[pl.ds(0, (PAIR_DEV - 1) * BIAS_ROWS)], 1)

        @pl.when(jnp.logical_not(right_lead_self))
        def _():
            wait_send(right_in.at[pl.ds(0, BIAS_ROWS)], 1)

    wait_send(left_in.at[pl.ds(0, (ATOM_DEV - 1) * BIAS_ROWS)], 2)

    @pl.when(left_lead)
    def _():
        wait_send(left_in.at[pl.ds(0, ATOM_DEV * BIAS_ROWS)], 3)

    wait_send(edge_out.at[1, pl.ds(0, DEV - 1)], 4)
    for step in range(4):
        sent = pl.ds(0, CHUNK - 1 if step == 0 else CHUNK)
        wait_send(edge_out.at[0, sent], 13 + step)
        wait_send(gp_out.at[sent], 17 + step)
    wait_send(prod_in.at[pl.ds(0, DEV - 1)], 5)
    for side in range(2):
        wait_send(grad_in.at[side, pl.ds(0, DEV - 1)], 7 + side)
    wait_send(row_msg.at[pl.ds(0, ATOM_DEV - 1), used], 9)

    @pl.when(row_lead)
    def _():
        wait_send(row_msg.at[pl.ds(0, 1), used], 10)

    wait_send(col_msg.at[pl.ds(0, PAIR_DEV - 1), used], 11)

    @pl.when(block != y)
    def _():
        wait_send(col_msg.at[pl.ds(0, 1), used], 11)

    @pl.when(col_lead & jnp.logical_not(col_lead_self))
    def _():
        wait_send(col_msg.at[pl.ds(0, 1), used], 12)


def hand_over(pair_in, atom_in, pair_out, atom_out, pair_held, atom_held, in_sems, out_sems):
    part = ROWS // PARTS
    blocks = [
        (pair_in.at[run], pair_held.at[run], pair_out.at[run])
        for run in (pl.ds(n * part, part) for n in range(PARTS))
    ]
    blocks.append((atom_in, atom_held, atom_out))
    loads = [
        pltpu.make_async_copy(src, held, in_sems.at[n]) for n, (src, held, _) in enumerate(blocks)
    ]
    stores = [
        pltpu.make_async_copy(held, dst, out_sems.at[n]) for n, (_, held, dst) in enumerate(blocks)
    ]
    for load in loads:
        load.start()
    for load, store in zip(loads, stores):
        load.wait()
        store.start()
    for store in stores:
        store.wait()


def body(
    pair_state,
    cotangent,
    atom_feats,
    atom_token,
    window_count,
    input_weight,
    output_weight,
    atom_weight,
    left_weight,
    right_weight,
):
    vmem = pl.BlockSpec(memory_space=pltpu.VMEM)
    hbm = pl.BlockSpec(memory_space=pl.ANY)
    rows = (ROWS, CH, COLS)
    scratch = [
        (rows, BF16),
        (rows, BF16),
        ((DEV, CH), BF16),
        ((1, DEV), jnp.int32),
        ((CH, 5 * CH), BF16),
        ((CH, CH), BF16),
        ((CH, 3 * CH), BF16),
        ((3 * CH, CH), BF16),
        ((3 * CH, CH), BF16),
        ((8, DEV), F32),
        ((DEV, 3 * CH), F32),
        ((2, 8, CH), F32),
        (((PAIR_DEV + 1) * 8 + 8, CH), F32),
        (((ATOM_DEV + 1) * 8 + 8, CH), F32),
        ((COLS, CH), F32),
        ((COLS, CH), F32),
        ((ROWS, CH), F32),
        ((ROWS, CH), F32),
        ((2, 4, 2, 2 * CHUNK, CH), BF16),
        ((CH, CH), BF16),
        ((CH, CH), BF16),
        (rows, F32),
        ((ROWS, COLS), F32),
        (rows, BF16),
        (rows, F32),
        (rows, F32),
        (rows, F32),
        (rows, F32),
        (rows, F32),
        ((CH * ROWS, COLS), F32),
        (rows, BF16),
        ((CH * ROWS, COLS), F32),
        ((CH * ROWS, COLS), F32),
        ((2, DEV, ROWS, COLS), BF16),
        ((2, 4, TOK, COLS), BF16),
        ((4, TOK, COLS), BF16),
        ((DEV, ROWS, COLS), BF16),
        ((DEV, ROWS, COLS), BF16),
        ((4, TOK, COLS), BF16),
        ((2, 4, TOK, COLS), BF16),
        ((2, DEV, ROWS, COLS), BF16),
        (rows, BF16),
        ((COLS, CH), F32),
        ((40, CH), F32),
        ((152, CH), F32),
        ((ATOM_DEV + 1, 8, CH), F32),
        ((PAIR_DEV + 1, 8, CH), F32),
        ((2 * ATOM_DEV, 8, CH), F32),
        ((2 * PAIR_DEV, 8, CH), F32),
    ]
    grads = pl.pallas_call(
        kernel,
        out_shape=(
            jax.ShapeDtypeStruct(pair_state.shape, BF16),
            jax.ShapeDtypeStruct(atom_feats.shape, BF16),
        ),
        in_specs=[hbm] * 4 + [pl.BlockSpec(memory_space=pltpu.SMEM)] + [hbm] * 5,
        out_specs=(hbm, vmem),
        scratch_shapes=[pltpu.VMEM(shape, dtype) for shape, dtype in scratch]
        + [pltpu.SemaphoreType.DMA((n,)) for n in (21, 21, 10)],
        compiler_params=pltpu.CompilerParams(
            collective_id=0, has_side_effects=True, vmem_limit_bytes=60 * 2**20
        ),
        cost_estimate=pl.CostEstimate(
            flops=1_700_000_000, bytes_accessed=2**21, transcendentals=2**20
        ),
    )(
        pair_state,
        cotangent,
        atom_feats,
        atom_token.reshape(1, -1),
        window_count,
        input_weight,
        output_weight,
        atom_weight,
        left_weight,
        right_weight,
    )
    return pl.pallas_call(
        hand_over,
        out_shape=tuple(jax.ShapeDtypeStruct(grad.shape, BF16) for grad in grads),
        in_specs=[hbm, hbm],
        out_specs=(hbm, hbm),
        scratch_shapes=[
            pltpu.VMEM((ROWS, COLS, CH), BF16),
            pltpu.VMEM((DEV, CH), BF16),
            pltpu.SemaphoreType.DMA((PARTS + 1,)),
            pltpu.SemaphoreType.DMA((PARTS + 1,)),
        ],
        compiler_params=pltpu.CompilerParams(vmem_limit_bytes=60 * 2**20),
    )(*grads)


def solution(mesh):
    placed = (
        P("pair", "atom", None),
        P("pair", "atom", None),
        P(("pair", "atom"), None),
        P(("pair", "atom")),
        P(("pair", "atom")),
        P(),
        P(),
        P(),
        P(),
        P(),
    )
    return jax.shard_map(
        body,
        mesh=mesh,
        in_specs=placed,
        out_specs=(P("pair", "atom", None), P(("pair", "atom"), None)),
        check_vma=False,
    )
```

```python
import jax
import jax.numpy as jnp
from jax import lax
from jax.experimental import pallas as pl
from jax.experimental.pallas import tpu as pltpu
from jax.sharding import PartitionSpec as P

EPSILON = 1e-05
F32 = jnp.float32
BF16 = jnp.bfloat16
ROWS = 16
COLS = 128
CH = 128
DEV = 128
TOK = 512
WIN = 32
PAIR_DEV = 32
ATOM_DEV = 4
CHUNK = 32
UNROLL = 16
BIAS_ROWS = 6
SUM_ROWS = 5
PARTS = 4


def dot_nn(a, b):
    return lax.dot_general(a, b, (((1,), (0,)), ((), ())), preferred_element_type=F32)


def dot_nt(a, b):
    return lax.dot_general(a, b, (((1,), (1,)), ((), ())), preferred_element_type=F32)


def dot_tn(a, b):
    return lax.dot_general(a, b, (((0,), (0,)), ((), ())), preferred_element_type=F32)


def split(x):
    high = x.astype(BF16)
    return high, (x - high.astype(F32)).astype(BF16)


def sigmoid(x):
    return 0.5 * jnp.tanh(0.5 * x) + 0.5


def loop(start, stop, step, unroll=1):
    def run(i, carry):
        step(i)
        return carry

    lax.fori_loop(start, stop, run, 0, unroll=unroll)


def kernel(
    pair_hbm,
    cot_hbm,
    feat_hbm,
    tok_hbm,
    count_ref,
    iw_hbm,
    ow_hbm,
    aw_hbm,
    lw_hbm,
    rw_hbm,
    pg_hbm,
    ag_ref,
    pair_ref,
    cot_ref,
    feat_ref,
    tok_ref,
    iw_ref,
    ow_ref,
    aw_ref,
    lw_ref,
    rw_ref,
    member_ref,
    dsilu_ref,
    bias_msg,
    right_in,
    left_in,
    right_bias,
    right_inv,
    left_bias,
    left_inv,
    wt_ref,
    wt5_ref,
    mt_ref,
    normed_ref,
    inv_ref,
    hidden_ref,
    sig_left,
    sig_right,
    der_left,
    der_right,
    gate_ref,
    gn_ref,
    gg_ref,
    work_a,
    work_b,
    edge_out,
    edge_in,
    prod_out,
    prod_in,
    gp_out,
    gp_in,
    grad_out,
    grad_in,
    pg_ref,
    col_acc,
    row_ext,
    col_ext,
    row_msg,
    col_msg,
    row_in,
    col_in,
    send_sem,
    recv_sem,
    load_sem,
):
    pos = lax.axis_index("pair")
    y = lax.axis_index("atom")
    me = pos * ATOM_DEV + y
    z = pos // 8
    x = (pos // 2) % 4
    c = pos % 2

    def remote(src, dst, sem, p, a):
        pltpu.make_async_remote_copy(
            src_ref=src,
            dst_ref=dst,
            send_sem=send_sem.at[sem],
            recv_sem=recv_sem.at[sem],
            device_id=(p, a),
            device_id_type=pl.DeviceIdType.MESH,
        ).start()

    def local(src, dst, sem):
        pltpu.make_async_copy(src, dst, recv_sem.at[sem]).start()

    def either(src, dst, sem, p, a, is_self):
        @pl.when(is_self)
        def _():
            local(src, dst, sem)

        @pl.when(jnp.logical_not(is_self))
        def _():
            remote(src, dst, sem, p, a)

    def wait_recv(ref, sem):
        pltpu.make_async_copy(ref, ref, recv_sem.at[sem]).wait()

    def wait_send(ref, sem):
        pltpu.make_async_copy(ref, ref, send_sem.at[sem]).wait()

    def channel(p, a):
        return ((p // 8 + (p // 2) % 4) % 4) * CHUNK + ((p // 2) % 4) * 8 + a * 2 + p % 2

    mine = channel(pos, y)
    group = (z + x) % 4

    def send_group(step, send_one, self_one):
        def one(q):
            xs = (x + (q // 2) % 4) % 4
            p = ((group + step + 4 - xs) % 4) * 8 + xs * 2 + (c + q % 2) % 2
            send_one(p, (y + q // 8) % 4)

        if step % 4 == 0:
            self_one()
            loop(1, CHUNK, one)
        else:
            loop(0, CHUNK, one)

    def group_rows(zc):
        return [
            pl.ds(pl.multiple_of((((zc + 4 - xs) % 4) * 8 + xs * 2) * ROWS, 2 * ROWS), 2 * ROWS)
            for xs in range(4)
        ]

    loads = [
        pltpu.make_async_copy(src, dst, load_sem.at[n])
        for n, (src, dst) in enumerate(
            (
                (feat_hbm, feat_ref),
                (aw_hbm, aw_ref),
                (tok_hbm, tok_ref),
                (lw_hbm, lw_ref),
                (rw_hbm, rw_ref),
                (iw_hbm, iw_ref),
                (ow_hbm, ow_ref),
                (pair_hbm, pair_ref),
                (cot_hbm, cot_ref),
            )
        )
    ]
    for load in loads:
        load.start()
    barrier = pltpu.get_barrier_semaphore()
    block = me // PAIR_DEV
    place = me % PAIR_DEV
    lead_right = ((place == 0) & (me > 0)).astype(jnp.int32)
    lead_left = ((y == 0) & (pos > 0)).astype(jnp.int32)

    def greet(to):
        @pl.when(to != me)
        def _():
            pl.semaphore_signal(
                barrier,
                inc=1,
                device_id=(to // ATOM_DEV, to % ATOM_DEV),
                device_id_type=pl.DeviceIdType.MESH,
            )

    loop(0, PAIR_DEV, lambda q: greet(y * PAIR_DEV + (place + q) % PAIR_DEV))
    loop(1, ATOM_DEV, lambda q: greet(pos * ATOM_DEV + (y + q) % ATOM_DEV))
    loop(0, ATOM_DEV, lambda q: greet(q * PAIR_DEV + pos))

    @pl.when(y < ATOM_DEV - 1)
    def _():
        greet((y + 1) * PAIR_DEV)

    @pl.when(pos < PAIR_DEV - 1)
    def _():
        greet((pos + 1) * ATOM_DEV)

    greeted = (
        PAIR_DEV
        - (block == y).astype(jnp.int32)
        + ATOM_DEV
        - 1
        + ATOM_DEV
        - (place == pos).astype(jnp.int32)
        + lead_right * (PAIR_DEV - (block == y + 1).astype(jnp.int32))
        + lead_left * ATOM_DEV
    )

    for load in loads[:5]:
        load.wait()

    atom_pre = dot_nn(feat_ref[...], aw_ref[...])
    atom_sig = sigmoid(atom_pre)
    atom_hidden = (atom_pre * atom_sig).astype(BF16)
    dsilu_ref[...] = atom_sig * (1.0 + atom_pre * (1.0 - atom_sig))
    slot = lax.broadcasted_iota(jnp.int32, (1, DEV), 1)
    live_count = jnp.full((1, DEV), 0, jnp.int32)
    for w in range(4):
        live_count = jnp.where(slot // WIN == w, count_ref[w], live_count)
    live = slot % WIN < live_count
    row8 = lax.broadcasted_iota(jnp.int32, (8, DEV), 0)
    lane8 = lax.broadcasted_iota(jnp.int32, (8, DEV), 1)
    member = jnp.where(
        (tok_ref[...] == me * 4 - 1 + row8) & (row8 < 5) & live, F32(1.0), F32(0.0)
    )
    member_ref[...] = member
    high, low = split(dot_nn(member.astype(BF16), atom_hidden))
    counts = jnp.sum(member, axis=1, keepdims=True)
    count_row = jnp.sum(jnp.where(lane8 == row8, counts, 0.0), axis=0, keepdims=True)
    for n, w_ref in enumerate((lw_ref, rw_ref)):
        weight = w_ref[...]
        sums = dot_nn(high, weight) + dot_nn(low, weight)
        bias_msg[n] = jnp.where(row8 == 5, count_row, sums)

    pl.semaphore_wait(barrier, greeted)

    right_src = bias_msg.at[1, pl.ds(0, BIAS_ROWS)]
    right_dst = right_in.at[pl.ds(pl.multiple_of(place * 8, 8), BIAS_ROWS)]
    right_self = block == y
    either(right_src, right_dst, 0, pos, block, right_self)
    loop(1, PAIR_DEV, lambda q: remote(right_src, right_dst, 0, (pos + q) % PAIR_DEV, block))
    right_lead = (place == 0) & (me > 0)
    right_lead_self = right_lead & (block - 1 == y)

    @pl.when(right_lead)
    def _():
        lead_dst = right_in.at[pl.ds(PAIR_DEV * 8, BIAS_ROWS)]
        either(right_src, lead_dst, 1, pos, block - 1, block - 1 == y)
        loop(
            1, PAIR_DEV, lambda q: remote(right_src, lead_dst, 1, (pos + q) % PAIR_DEV, block - 1)
        )

    left_src = bias_msg.at[0, pl.ds(0, BIAS_ROWS)]
    left_dst = left_in.at[pl.ds(pl.multiple_of(y * 8, 8), BIAS_ROWS)]
    local(left_src, left_dst, 2)
    loop(1, ATOM_DEV, lambda q: remote(left_src, left_dst, 2, pos, (y + q) % ATOM_DEV))
    left_lead = (y == 0) & (pos > 0)

    @pl.when(left_lead)
    def _():
        loop(
            0,
            ATOM_DEV,
            lambda q: remote(
                left_src,
                left_in.at[pl.ds(ATOM_DEV * 8, BIAS_ROWS)],
                3,
                pos - 1,
                (y + q) % ATOM_DEV,
            ),
        )

    for load in loads[5:]:
        load.wait()
    for q in range(4):
        turned = iw_ref[:, q * CH : (q + 1) * CH].astype(F32).T.astype(BF16)
        for zc in range(4):
            part = turned[zc * CHUNK : (zc + 1) * CHUNK, :]
            at = slice((q % 2) * CHUNK, (q % 2 + 1) * CHUNK)
            wt_ref[q // 2, zc, 0, at, :] = part
            wt_ref[q // 2, (zc + 3) % 4, 1, at, :] = part
    wt5_ref[...] = iw_ref[:, 4 * CH :].astype(F32).T.astype(BF16)
    mt_ref[...] = ow_ref[...].astype(F32).T.astype(BF16)

    @pl.when(y == ATOM_DEV - 1)
    def _():
        right_in[pl.ds(PAIR_DEV * 8, 8), :] = jnp.zeros((8, CH), F32)

    @pl.when(pos == PAIR_DEV - 1)
    def _():
        left_in[pl.ds(ATOM_DEV * 8, 8), :] = jnp.zeros((8, CH), F32)

    wait_recv(right_in.at[pl.ds(0, PAIR_DEV * BIAS_ROWS)], 0)

    @pl.when(y < ATOM_DEV - 1)
    def _():
        wait_recv(right_in.at[pl.ds(PAIR_DEV * 8, BIAS_ROWS)], 1)

    wait_recv(left_in.at[pl.ds(0, ATOM_DEV * BIAS_ROWS)], 2)

    @pl.when(pos < PAIR_DEV - 1)
    def _():
        wait_recv(left_in.at[pl.ds(ATOM_DEV * 8, BIAS_ROWS)], 3)


    def finish_bias(src, bias_ref, inverse_ref, n):
        lane = lax.broadcasted_iota(jnp.int32, (n, CH), 1)
        count_own = src[pl.ds(5, n, stride=8), :]
        count_next = src[pl.ds(13, n, stride=8), :]
        for q in range(4):
            total = src[pl.ds(1 + q, n, stride=8), :]
            number = jnp.where(lane == 1 + q, count_own, 0.0)
            if q == 3:
                total = total + src[pl.ds(8, n, stride=8), :]
                number = number + jnp.where(lane == 0, count_next, 0.0)
            inverse = 1.0 / jnp.sum(number, axis=1, keepdims=True)
            bias_ref[pl.ds(q, n, stride=4), :] = (total * inverse).astype(BF16).astype(F32)
            inverse_ref[pl.ds(q, n, stride=4), :] = jnp.broadcast_to(inverse, (n, CH))

    finish_bias(right_in, right_bias, right_inv, PAIR_DEV)
    finish_bias(left_in, left_bias, left_inv, ATOM_DEV)


    def front(r):
        values = pair_ref[r].astype(F32) + left_bias[pl.ds(r, 1), :] + right_bias[...]
        values = values.T
        centre = jnp.mean(values, axis=0, keepdims=True)
        shifted = values - centre
        inverse = lax.rsqrt(jnp.mean(shifted * shifted, axis=0, keepdims=True) + EPSILON)
        normed = shifted * inverse
        normed_ref[r] = normed
        inv_ref[pl.ds(r, 1), :] = inverse
        hidden_ref[r] = normed.astype(BF16)

    loop(0, ROWS, front, UNROLL)


    rows_here = pl.ds(pl.multiple_of(pos * ROWS, ROWS), ROWS)
    for side, sig_ref, der_ref, work in (
        (1, sig_right, der_right, work_b),
        (0, sig_left, der_left, work_a),
    ):
        edge_dst = edge_in.at[side, y, rows_here]
        for half in range(2):
            groups = [(group + 2 * half + n) % 4 for n in range(2)]
            firsts = [pl.multiple_of(zc * CHUNK, CHUNK) for zc in groups]

            def edges(r):
                weight = wt_ref[side, groups[0]].reshape(4 * CHUNK, CH)
                pre = dot_nn(weight, hidden_ref[r])
                for n in range(2):
                    value = pre[2 * n * CHUNK : (2 * n + 1) * CHUNK]
                    opened = sigmoid(pre[(2 * n + 1) * CHUNK : (2 * n + 2) * CHUNK])
                    edge = opened * value
                    work[pl.ds(n * CHUNK * ROWS + r, CHUNK, stride=ROWS), :] = edge
                    sig_ref[r, pl.ds(firsts[n], CHUNK), :] = opened
                    der_ref[r, pl.ds(firsts[n], CHUNK), :] = edge * (1.0 - opened)

            loop(0, ROWS, edges, UNROLL)
            for n in range(2):
                edge_out[side, pl.ds(firsts[n], CHUNK)] = (
                    work[n * CHUNK * ROWS : (n + 1) * CHUNK * ROWS, :]
                    .reshape(CHUNK, ROWS, COLS)
                    .astype(BF16)
                )
                step = 2 * half + n
                sem = 4 if side == 1 else 13 + step
                send_group(
                    step,
                    lambda p, a: remote(edge_out.at[side, channel(p, a)], edge_dst, sem, p, a),
                    lambda: local(edge_out.at[side, mine], edge_dst, sem),
                )

    def gate(r):
        opened = sigmoid(dot_nn(wt5_ref[...], hidden_ref[r]))
        gated = cot_ref[r].astype(F32).T * opened
        gate_ref[r] = gated * (1.0 - opened)
        gn_ref[pl.ds(r, CH, stride=ROWS), :] = dot_nn(ow_ref[...], gated.astype(BF16))

    loop(0, ROWS, gate, UNROLL)

    def total(i, acc):
        chunk = gn_ref[pl.ds(pl.multiple_of(i * 128, 128), 128), :].reshape(8, ROWS, COLS)
        return acc + jnp.sum(chunk, axis=0)

    zero = jnp.zeros((ROWS, COLS), F32)
    gn_mean = lax.fori_loop(0, 16, total, zero) * (1.0 / CH)


    prod_dst = prod_in.at[mine]

    def block_of(ref, p, a):
        return ref.at[a, pl.ds(pl.multiple_of(p * ROWS, ROWS), ROWS)]

    wait_recv(edge_in.at[1], 4)
    for step in range(4):
        wait_recv(edge_in.at[0, 0], 13 + step)
        rows = group_rows((group + 4 - step) % 4)
        product = None
        for a in range(4):
            lhs = jnp.concatenate([edge_in[0, a, run, :] for run in rows], axis=0)
            term = dot_nt(lhs, edge_in[1, a])
            product = term if product is None else product + term
        product = product.astype(BF16)
        for a in range(4):
            for n, run in enumerate(rows):
                prod_out[a, run, :] = product[
                    2 * ROWS * n : 2 * ROWS * (n + 1), COLS * a : COLS * (a + 1)
                ]
        send_group(
            (4 - step) % 4,
            lambda p, a: remote(block_of(prod_out, p, a), prod_dst, 5, p, a),
            lambda: local(block_of(prod_out, pos, y), prod_dst, 5),
        )
    wait_recv(prod_in, 5)

    def sum_prod(i, acc):
        return acc + jnp.sum(prod_in[pl.ds(i * 8, 8)].astype(F32), axis=0)

    prod_mean = lax.fori_loop(0, 16, sum_prod, zero) * (1.0 / CH)

    def sum_squares(i, carry):
        squares, cross = carry
        shifted = prod_in[pl.ds(i * 8, 8)].astype(F32) - prod_mean[None]
        upstream = gn_ref[pl.ds(pl.multiple_of(i * 128, 128), 128), :].reshape(8, ROWS, COLS)
        return (
            squares + jnp.sum(shifted * shifted, axis=0),
            cross + jnp.sum(upstream * shifted, axis=0),
        )

    squares, cross = lax.fori_loop(0, 16, sum_squares, (zero, zero))
    prod_inv = lax.rsqrt(squares * (1.0 / CH) + EPSILON)
    cross = cross * prod_inv * prod_inv * (1.0 / CH)


    gp_dst = gp_in.at[y, rows_here]
    for step in range(4):
        zc = (group + step) % 4

        def grads(i):
            at = zc * CHUNK + i * 8
            shifted = prod_in[pl.ds(at, 8)].astype(F32) - prod_mean[None]
            upstream = gn_ref[pl.ds(pl.multiple_of(at * ROWS, 128), 128), :]
            upstream = upstream.reshape(8, ROWS, COLS)
            grad = prod_inv[None] * (upstream - gn_mean[None] - shifted * cross[None])
            gp_out[pl.ds(at, 8)] = grad.astype(BF16)

        loop(0, 4, grads, 4)
        send_group(
            step,
            lambda p, a: remote(gp_out.at[channel(p, a)], gp_dst, 17 + step, p, a),
            lambda: local(gp_out.at[mine], gp_dst, 17 + step),
        )


    left_dst = grad_in.at[0, mine]
    for step in range(4):
        wait_recv(gp_in.at[0], 17 + step)
        rows = group_rows((group + 4 - step) % 4)
        lhs = jnp.concatenate(
            [jnp.concatenate([gp_in[a, run, :] for run in rows], axis=0) for a in range(4)], axis=1
        )
        for a in range(4):
            grad = dot_nn(lhs, edge_in[1, a]).astype(BF16)
            for n, run in enumerate(rows):
                grad_out[0, a, run, :] = grad[2 * ROWS * n : 2 * ROWS * (n + 1), :]
        send_group(
            (4 - step) % 4,
            lambda p, a: remote(block_of(grad_out.at[0], p, a), left_dst, 7, p, a),
            lambda: local(block_of(grad_out.at[0], pos, y), left_dst, 7),
        )
    for zc in range(4):
        lhs = gp_in[zc].T
        for a in range(4):
            grad_out[1, a, 128 * zc : 128 * (zc + 1), :] = dot_nn(lhs, edge_in[0, a]).astype(BF16)
    right_dst = grad_in.at[1, mine]
    for step in range(4):
        send_group(
            step,
            lambda p, a: remote(block_of(grad_out.at[1], p, a), right_dst, 8, p, a),
            lambda: local(block_of(grad_out.at[1], pos, y), right_dst, 8),
        )

    def lay_normed(i):
        shifted = (prod_in[pl.ds(i * 8, 8)].astype(F32) - prod_mean[None]) * prod_inv[None]
        work_a[pl.ds(pl.multiple_of(i * 128, 128), 128), :] = shifted.reshape(128, COLS)

    loop(0, 16, lay_normed, UNROLL)

    def gate_grad(r):
        normed = work_a[pl.ds(r, CH, stride=ROWS), :].astype(BF16)
        gg_ref[r] = (dot_nn(mt_ref[...], normed) * gate_ref[r]).astype(BF16)

    loop(0, ROWS, gate_grad, UNROLL)


    row_ext[...] = jnp.zeros_like(row_ext)
    col_ext[...] = jnp.zeros_like(col_ext)
    col_acc[...] = jnp.zeros_like(col_acc)

    def lay_grads(side, work):
        def lay(i):
            work[pl.ds(pl.multiple_of(i * 128, 128), 128), :] = (
                grad_in[side, pl.ds(i * 8, 8)].astype(F32).reshape(128, COLS)
            )

        loop(0, 16, lay, UNROLL)

    def branches(work, sig_ref, der_ref, r):
        flow = work[pl.ds(r, CH, stride=ROWS), :]
        return [(flow * sig_ref[r]).astype(BF16), (flow * der_ref[r]).astype(BF16)]

    def partial(r):
        left = branches(work_a, sig_left, der_left, r)
        gate_ref[r] = dot_nn(iw_ref[:, : 2 * CH], jnp.concatenate(left, axis=0)) + dot_nn(
            iw_ref[:, 4 * CH :], gg_ref[r]
        )

    wait_recv(grad_in.at[0], 7)
    lay_grads(0, work_a)
    loop(0, ROWS, partial, UNROLL)
    wait_recv(grad_in.at[1], 8)
    lay_grads(1, work_b)

    def last(r):
        right = branches(work_b, sig_right, der_right, r)
        grad = gate_ref[r] + dot_nn(iw_ref[:, 2 * CH : 4 * CH], jnp.concatenate(right, axis=0))
        normed = normed_ref[r]
        first_mean = jnp.mean(grad, axis=0, keepdims=True)
        cross_mean = jnp.mean(grad * normed, axis=0, keepdims=True)
        grad = inv_ref[pl.ds(r, 1), :] * (grad - first_mean - normed * cross_mean)
        grad = grad.T
        pg_ref[r] = grad.astype(BF16)
        col_acc[...] += grad
        row_ext[pl.ds(8 + r, 1), :] = jnp.sum(grad, axis=0, keepdims=True)

    loop(0, ROWS, last, UNROLL)


    store = pltpu.make_async_copy(pg_ref, pg_hbm, load_sem.at[9])
    store.start()

    row_ext[8:24, :] = row_ext[8:24, :] * left_inv[...]
    col_ext[8:136, :] = col_acc[...] * right_inv[...]
    for m in range(ATOM_DEV + 1):
        row_msg[m] = row_ext[7 + 4 * m : 15 + 4 * m, :]
    for m in range(PAIR_DEV + 1):
        col_msg[m] = col_ext[7 + 4 * m : 15 + 4 * m, :]

    used = pl.ds(0, SUM_ROWS)
    local(row_msg.at[y, used], row_in.at[y, used], 9)

    def send_row(q):
        a = (y + q) % ATOM_DEV
        remote(row_msg.at[a, used], row_in.at[y, used], 9, pos, a)

    loop(1, ATOM_DEV, send_row)
    row_lead = pos < PAIR_DEV - 1

    @pl.when(row_lead)
    def _():
        remote(row_msg.at[ATOM_DEV, used], row_in.at[ATOM_DEV + y, used], 10, pos + 1, 0)

    def send_col(q):
        m = (place + q) % PAIR_DEV
        p = y * 8 + m // 4
        a = m % 4
        either(col_msg.at[m, used], col_in.at[pos, used], 11, p, a, (p == pos) & (a == y))

    loop(0, PAIR_DEV, send_col)
    col_lead = y < ATOM_DEV - 1
    col_lead_self = col_lead & (pos == (y + 1) * 8) & (y == 0)

    @pl.when(col_lead)
    def _():
        either(
            col_msg.at[PAIR_DEV, used],
            col_in.at[PAIR_DEV + pos, used],
            12,
            (y + 1) * 8,
            0,
            col_lead_self,
        )

    row_more = (y == 0) & (pos > 0)
    col_more = (place == 0) & (me > 0)

    @pl.when(jnp.logical_not(row_more))
    def _():
        row_in[ATOM_DEV:] = jnp.zeros((ATOM_DEV, 8, CH), F32)

    @pl.when(jnp.logical_not(col_more))
    def _():
        col_in[PAIR_DEV:] = jnp.zeros((PAIR_DEV, 8, CH), F32)

    wait_recv(row_in.at[pl.ds(0, ATOM_DEV), used], 9)

    @pl.when(row_more)
    def _():
        wait_recv(row_in.at[pl.ds(ATOM_DEV, ATOM_DEV), used], 10)

    wait_recv(col_in.at[pl.ds(0, PAIR_DEV), used], 11)

    @pl.when(col_more)
    def _():
        wait_recv(col_in.at[pl.ds(PAIR_DEV, PAIR_DEV), used], 12)


    single = jnp.zeros((8, 3 * CH), F32)
    for ref, w_ref in ((row_in, lw_ref), (col_in, rw_ref)):
        weight = w_ref[...]
        sums = jnp.where(row8 < SUM_ROWS, jnp.sum(ref[...], axis=0), 0.0)
        for part in split(sums):
            single = single + dot_nt(part, weight)
    picked = dot_tn(member_ref[...].astype(BF16), single.astype(BF16))
    atom_grad = (picked * dsilu_ref[...]).astype(BF16)
    ag_ref[...] = dot_nt(atom_grad, aw_ref[...]).astype(BF16)

    store.wait()

    wait_send(right_in.at[pl.ds(0, (PAIR_DEV - 1) * BIAS_ROWS)], 0)

    @pl.when(jnp.logical_not(right_self))
    def _():
        wait_send(right_in.at[pl.ds(0, BIAS_ROWS)], 0)

    @pl.when(right_lead)
    def _():
        wait_send(right_in.at[pl.ds(0, (PAIR_DEV - 1) * BIAS_ROWS)], 1)

        @pl.when(jnp.logical_not(right_lead_self))
        def _():
            wait_send(right_in.at[pl.ds(0, BIAS_ROWS)], 1)

    wait_send(left_in.at[pl.ds(0, (ATOM_DEV - 1) * BIAS_ROWS)], 2)

    @pl.when(left_lead)
    def _():
        wait_send(left_in.at[pl.ds(0, ATOM_DEV * BIAS_ROWS)], 3)

    wait_send(edge_out.at[1, pl.ds(0, DEV - 1)], 4)
    for step in range(4):
        sent = pl.ds(0, CHUNK - 1 if step == 0 else CHUNK)
        wait_send(edge_out.at[0, sent], 13 + step)
        wait_send(gp_out.at[sent], 17 + step)
    wait_send(prod_in.at[pl.ds(0, DEV - 1)], 5)
    for side in range(2):
        wait_send(grad_in.at[side, pl.ds(0, DEV - 1)], 7 + side)
    wait_send(row_msg.at[pl.ds(0, ATOM_DEV - 1), used], 9)

    @pl.when(row_lead)
    def _():
        wait_send(row_msg.at[pl.ds(0, 1), used], 10)

    wait_send(col_msg.at[pl.ds(0, PAIR_DEV - 1), used], 11)

    @pl.when(block != y)
    def _():
        wait_send(col_msg.at[pl.ds(0, 1), used], 11)

    @pl.when(col_lead & jnp.logical_not(col_lead_self))
    def _():
        wait_send(col_msg.at[pl.ds(0, 1), used], 12)


def hand_over(pair_in, atom_in, pair_out, atom_out, pair_held, atom_held, in_sems, out_sems):
    part = ROWS // PARTS
    blocks = [
        (pair_in.at[run], pair_held.at[run], pair_out.at[run])
        for run in (pl.ds(n * part, part) for n in range(PARTS))
    ]
    blocks.append((atom_in, atom_held, atom_out))
    loads = [
        pltpu.make_async_copy(src, held, in_sems.at[n]) for n, (src, held, _) in enumerate(blocks)
    ]
    stores = [
        pltpu.make_async_copy(held, dst, out_sems.at[n]) for n, (_, held, dst) in enumerate(blocks)
    ]
    for load in loads:
        load.start()
    for load, store in zip(loads, stores):
        load.wait()
        store.start()
    for store in stores:
        store.wait()


def body(
    pair_state,
    cotangent,
    atom_feats,
    atom_token,
    window_count,
    input_weight,
    output_weight,
    atom_weight,
    left_weight,
    right_weight,
):
    vmem = pl.BlockSpec(memory_space=pltpu.VMEM)
    hbm = pl.BlockSpec(memory_space=pl.ANY)
    rows = (ROWS, CH, COLS)
    scratch = [
        (rows, BF16),
        (rows, BF16),
        ((DEV, CH), BF16),
        ((1, DEV), jnp.int32),
        ((CH, 5 * CH), BF16),
        ((CH, CH), BF16),
        ((CH, 3 * CH), BF16),
        ((3 * CH, CH), BF16),
        ((3 * CH, CH), BF16),
        ((8, DEV), F32),
        ((DEV, 3 * CH), F32),
        ((2, 8, CH), F32),
        (((PAIR_DEV + 1) * 8 + 8, CH), F32),
        (((ATOM_DEV + 1) * 8 + 8, CH), F32),
        ((COLS, CH), F32),
        ((COLS, CH), F32),
        ((ROWS, CH), F32),
        ((ROWS, CH), F32),
        ((2, 4, 2, 2 * CHUNK, CH), BF16),
        ((CH, CH), BF16),
        ((CH, CH), BF16),
        (rows, F32),
        ((ROWS, COLS), F32),
        (rows, BF16),
        (rows, F32),
        (rows, F32),
        (rows, F32),
        (rows, F32),
        (rows, F32),
        ((CH * ROWS, COLS), F32),
        (rows, BF16),
        ((CH * ROWS, COLS), F32),
        ((CH * ROWS, COLS), F32),
        ((2, DEV, ROWS, COLS), BF16),
        ((2, 4, TOK, COLS), BF16),
        ((4, TOK, COLS), BF16),
        ((DEV, ROWS, COLS), BF16),
        ((DEV, ROWS, COLS), BF16),
        ((4, TOK, COLS), BF16),
        ((2, 4, TOK, COLS), BF16),
        ((2, DEV, ROWS, COLS), BF16),
        (rows, BF16),
        ((COLS, CH), F32),
        ((40, CH), F32),
        ((152, CH), F32),
        ((ATOM_DEV + 1, 8, CH), F32),
        ((PAIR_DEV + 1, 8, CH), F32),
        ((2 * ATOM_DEV, 8, CH), F32),
        ((2 * PAIR_DEV, 8, CH), F32),
    ]
    grads = pl.pallas_call(
        kernel,
        out_shape=(
            jax.ShapeDtypeStruct(pair_state.shape, BF16),
            jax.ShapeDtypeStruct(atom_feats.shape, BF16),
        ),
        in_specs=[hbm] * 4 + [pl.BlockSpec(memory_space=pltpu.SMEM)] + [hbm] * 5,
        out_specs=(hbm, vmem),
        scratch_shapes=[pltpu.VMEM(shape, dtype) for shape, dtype in scratch]
        + [pltpu.SemaphoreType.DMA((n,)) for n in (21, 21, 10)],
        compiler_params=pltpu.CompilerParams(
            collective_id=0, has_side_effects=True, vmem_limit_bytes=60 * 2**20
        ),
        cost_estimate=pl.CostEstimate(
            flops=1_700_000_000, bytes_accessed=2**21, transcendentals=2**20
        ),
    )(
        pair_state,
        cotangent,
        atom_feats,
        atom_token.reshape(1, -1),
        window_count,
        input_weight,
        output_weight,
        atom_weight,
        left_weight,
        right_weight,
    )
    return pl.pallas_call(
        hand_over,
        out_shape=tuple(jax.ShapeDtypeStruct(grad.shape, BF16) for grad in grads),
        in_specs=[hbm, hbm],
        out_specs=(hbm, hbm),
        scratch_shapes=[
            pltpu.VMEM((ROWS, COLS, CH), BF16),
            pltpu.VMEM((DEV, CH), BF16),
            pltpu.SemaphoreType.DMA((PARTS + 1,)),
            pltpu.SemaphoreType.DMA((PARTS + 1,)),
        ],
        compiler_params=pltpu.CompilerParams(vmem_limit_bytes=60 * 2**20),
    )(*grads)


def solution(mesh):
    placed = (
        P("pair", "atom", None),
        P("pair", "atom", None),
        P(("pair", "atom"), None),
        P(("pair", "atom")),
        P(("pair", "atom")),
        P(),
        P(),
        P(),
        P(),
        P(),
    )
    return jax.shard_map(
        body,
        mesh=mesh,
        in_specs=placed,
        out_specs=(P("pair", "atom", None), P(("pair", "atom"), None)),
        check_vma=False,
    )
```
